256 devices in a mesh: ia: 16 (over z, y_lo), ja: 16 (over y_hi, x, core).
Axes of the slice: x: 4, y: 4 (y_hi: 2, y_lo: 2; y = y_hi * 2 + y_lo), z: 8, core: 2. Of those that a mesh axis runs over, the one named last changes fastest.
Arguments:
- amplitudes: float32 [64, 64, 384, 384], P('ia', 'ja'), may hold values from -6 to 6
- integrals: float32 [768, 384, 384], P('ia', 'ja'), may hold values from -0.0625 to 0.0625
- occ_irrep: int32 [64], replicated, may hold values from 0 to 7
- vir_irrep: int32 [6], replicated, may hold values from 0 to 7
- occ_energy: float32 [64], replicated, may hold values from -2 to -0.3
- vir_energy: float32 [384], replicated, may hold values from 0.2 to 2.5
Outputs:
- residual: float32 [64, 64, 768], P('ia', None, 'ja')
The draws below stay inside these ranges and needn't reach their ends.
All inputs are finite; a program needn't handle non-finite values.
Results may differ from the reference program's by a relative error of at most 0.0003.
Values sent between devices are 32-bit elements; how exact they have to be, the bound alone decides.
No kernel may reach another device: no remote copies, remote signals or barrier semaphores. Data moves between devices by JAX's collectives and lax.ppermute only.
A program may use at most 192 MiB of HBM per device.

```python
import jax
import jax.numpy as jnp
from jax import lax

O = 64
NV = 384
VT = 64
SA = 2
NVT = 6
NAB = 768


def touch_ends(drawn, stream_key, least, largest):
    extent = drawn.shape
    spot = [jax.random.randint(jax.random.fold_in(stream_key, axis), (), 0, extent[axis]) for axis in range(len(extent))]
    drawn = drawn.at[tuple(spot)].set(least)
    longest = extent.index(max(extent))
    spot[longest] = (spot[longest] + 1) % extent[longest]
    return drawn.at[tuple(spot)].set(largest)


def shard_levels(own_key, dims, split, low, largest):
    def one(axis_at, blocks):
        steps = jax.random.uniform(jax.random.fold_in(jax.random.fold_in(own_key, 6), axis_at), (blocks,), jnp.float32, low / len(split), largest / len(split))
        return jnp.repeat(jnp.exp(steps), dims[axis_at] // blocks).reshape((-1,) + (1,) * (len(dims) - axis_at - 1))

    gain = one(*split[0])
    for cut in split[1:]:
        gain = gain * one(*cut)
    return gain


def centred(own_key, shape, scale, most, split=(), dtype=jnp.bfloat16):
    entries = jax.random.normal(own_key, shape, jnp.float32) * scale
    if len(split) > 0:
        entries = shard_levels(own_key, shape, split, -0.22, 0.18) * entries
    return jnp.clip(entries, min=-most, max=most).astype(dtype)


def setup_inputs(seed: int = 0) -> dict:
    streams_of = jax.random.split(jax.random.key(seed), 7)
    amplitudes = centred(streams_of[0], (O, O, NV, NV), 1.0, 6.0, ((0, 16), (1, 16)), jnp.float32)
    integrals = centred(streams_of[1], (NAB, NV, NV), (NV * NV // 16) ** -0.5, 0.0625, ((0, 16), (1, 16)), jnp.float32)
    occ_irrep = touch_ends(jax.random.randint(streams_of[2], (O,), 0, 8), jax.random.fold_in(streams_of[2], 1), 0, 7).astype(jnp.int32)
    vir_irrep = touch_ends(jax.random.randint(streams_of[3], (NVT,), 0, 8), jax.random.fold_in(streams_of[3], 1), 0, 7).astype(jnp.int32)
    occ_energy = jnp.clip(jax.random.uniform(streams_of[4], (O,), jnp.float32, -2.0, -0.3), -2.0, -0.3)
    vir_energy = jnp.clip(jax.random.uniform(streams_of[5], (NV,), jnp.float32, 0.2, 2.5), 0.2, 2.5)
    return dict(amplitudes=amplitudes, integrals=integrals, occ_irrep=occ_irrep, vir_irrep=vir_irrep, occ_energy=occ_energy, vir_energy=vir_energy)


def tile_labels(vir_irrep):
    return jnp.broadcast_to(vir_irrep[:, None], (NV // VT, VT)).reshape(NV)


def reference(amplitudes, integrals, occ_irrep, vir_irrep, occ_energy, vir_energy):
    orbital = tile_labels(vir_irrep)
    pair_cd = jnp.bitwise_xor(orbital[:, None], orbital[None, :])
    pair_ij = jnp.bitwise_xor(occ_irrep[:, None], occ_irrep[None, :])
    pair_ab = jnp.bitwise_xor(orbital[:SA, None], orbital[None, :]).reshape(SA * NV)
    masked_v = jnp.where(pair_ab[:, None, None] == pair_cd[None], integrals, 0.0).reshape(SA * NV, NV * NV)

    def ladder_row(inputs):
        amp_row, row_labels = inputs
        masked_t = jnp.where(row_labels[:, None, None] == pair_cd[None], amp_row, 0.0).reshape(O, NV * NV)
        return lax.dot_general(masked_t, masked_v, (((1,), (1,)), ((), ())), precision=lax.Precision.HIGHEST, preferred_element_type=jnp.float32)

    ladder = lax.map(ladder_row, (amplitudes, pair_ij))
    difference = ladder - jnp.transpose(ladder, (1, 0, 2))
    ab_energy = (vir_energy[:SA, None] + vir_energy[None, :]).reshape(SA * NV)
    denominator = (occ_energy[:, None, None] + occ_energy[None, :, None]) - ab_energy[None, None, :]
    return difference / denominator
```

```python
import functools

import jax
import jax.numpy as jnp
from jax import lax
from jax.experimental import pallas as pl
from jax.experimental.pallas import tpu as pltpu
from jax.sharding import Mesh, PartitionSpec as P

O = 64
NV = 384
VT = 64
SA = 2
NVT = NV // VT
Z = 8
YL = 2
JA = 16
NI = 4
PAIRS = NI * NI
CB = NV // JA
CK = CB // YL
AB = SA * NV // (Z * YL)
ROWS = JA * PAIRS
LANES = 128
VMEM_LIMIT = 60 * 1024 * 1024


def slot_tiles(wanted, vir, tile):
    lane = lax.broadcasted_iota(jnp.int32, wanted.shape, wanted.ndim - 1)
    slot = jnp.where(lane < VT, 2 * tile, 2 * tile + 1)
    count = jnp.zeros(wanted.shape, jnp.int32)
    chosen = jnp.full(wanted.shape, -1, jnp.int32)
    for td in range(NVT):
        match = wanted == vir[td]
        chosen = jnp.where(match & (count == slot), td, chosen)
        count = jnp.where(match, count + 1, count)
    return chosen


def pack_tiles(block, chosen_of):
    lane = lax.broadcasted_iota(jnp.int32, block.shape[:2] + (LANES,), 2)
    low = lane < VT
    packed = [jnp.zeros(block.shape[:2] + (LANES,), jnp.float32) for _ in chosen_of]
    for k in range(NV // LANES):
        part = block[:, :, k * LANES : (k + 1) * LANES]
        turned = pltpu.roll(part, VT, 2)
        even = jnp.where(low, part, turned)
        odd = jnp.where(low, turned, part)
        for t, chosen in enumerate(chosen_of):
            packed[t] = jnp.where(chosen == 2 * k, even, packed[t])
            packed[t] = jnp.where(chosen == 2 * k + 1, odd, packed[t])
    return packed


def pack_amplitudes_kernel(tiles, occ, vir, t_ref, out_ref, chosen_ref):
    step = pl.program_id(0)

    @pl.when(step == 0)
    def _():
        first_i = NI * (YL * lax.axis_index("z") + lax.axis_index("yl"))
        first_j = NI * lax.axis_index("ja")
        for p in range(PAIRS):
            label = occ[first_i + p // NI] ^ occ[first_j + p % NI]
            for tc in range(NVT):
                wanted = jnp.full((8, LANES), label ^ vir[tc], jnp.int32)
                for t in range(tiles):
                    chosen_ref[tc, t, p] = slot_tiles(wanted, vir, t)

    for b in range(CB // 8):
        tc = (step * (CB // 8) + b) // (VT // 8)
        block = t_ref[:, b * 8 : (b + 1) * 8, :]
        packed = pack_tiles(block, [chosen_ref[tc, t] for t in range(tiles)])
        for t in range(tiles):
            turned = jnp.swapaxes(packed[t], 0, 1)
            for r in range(8):
                c = b * 8 + r
                out_ref[c // CK, 0, c % CK, :, t * LANES : (t + 1) * LANES] = turned[r]


def pack_amplitudes(amplitudes, occ_irrep, vir_irrep, tiles):
    width = tiles * LANES
    return pl.pallas_call(
        functools.partial(pack_amplitudes_kernel, tiles),
        out_shape=jax.ShapeDtypeStruct((YL, JA, CK, PAIRS, width), jnp.float32),
        grid=(JA,),
        in_specs=[
            pl.BlockSpec(memory_space=pltpu.SMEM),
            pl.BlockSpec(memory_space=pltpu.SMEM),
            pl.BlockSpec((PAIRS, CB, NV), lambda s: (0, s, 0)),
        ],
        out_specs=pl.BlockSpec((YL, 1, CK, PAIRS, width), lambda s: (0, s, 0, 0, 0)),
        scratch_shapes=[pltpu.VMEM((NVT, tiles, PAIRS, 8, LANES), jnp.int32)],
        compiler_params=pltpu.CompilerParams(vmem_limit_bytes=VMEM_LIMIT),
        cost_estimate=pl.CostEstimate(flops=10**7, bytes_accessed=14 * 10**6, transcendentals=0),
    )(occ_irrep, vir_irrep, amplitudes.reshape(PAIRS, NV, NV))


def pack_integrals_kernel(tiles, vir, v_ref, out_ref):
    step = pl.program_id(0)
    ia = YL * lax.axis_index("z") + lax.axis_index("yl")
    tb = (AB * (ia % (Z * YL // SA)) + 16 * step) // VT
    for b in range(CB // 8):
        tc = (lax.axis_index("ja") * (CB // 8) + b) // (VT // 8)
        wanted = jnp.full((1, 8, LANES), vir[0] ^ vir[tb] ^ vir[tc], jnp.int32)
        packed = pack_tiles(v_ref[:, b * 8 : (b + 1) * 8, :], [slot_tiles(wanted, vir, t) for t in range(tiles)])
        for t in range(tiles):
            turned = jnp.swapaxes(packed[t], 0, 1)
            for r in range(8):
                c = b * 8 + r
                out_ref[c // CK, c % CK, :, t * LANES : (t + 1) * LANES] = turned[r]


def pack_integrals(integrals, vir_irrep, tiles):
    width = tiles * LANES
    return pl.pallas_call(
        functools.partial(pack_integrals_kernel, tiles),
        out_shape=jax.ShapeDtypeStruct((YL, CK, AB, width), jnp.float32),
        grid=(AB // 16,),
        in_specs=[
            pl.BlockSpec(memory_space=pltpu.SMEM),
            pl.BlockSpec((16, CB, NV), lambda s: (s, 0, 0)),
        ],
        out_specs=pl.BlockSpec((YL, CK, 16, width), lambda s: (0, 0, s, 0)),
        compiler_params=pltpu.CompilerParams(vmem_limit_bytes=VMEM_LIMIT),
        cost_estimate=pl.CostEstimate(flops=10**6, bytes_accessed=3 * 10**6, transcendentals=0),
    )(vir_irrep, integrals)


def split(values):
    high = values.astype(jnp.bfloat16)
    return high, (values - high.astype(jnp.float32)).astype(jnp.bfloat16)


RING = [(0, 0, 0), (0, 1, 0)]
RING += [(1 + 2 * s + d, h, (s + 1) * (1 - 2 * d)) for s in range(3) for d in range(2) for h in range(YL)]
RING += [(7, 0, 4), (8, 0, 4)]


def contract_kernel(vir, labels_ref, t_ref, *refs):
    v_refs, (out_ref, v_high, v_low) = refs[:9], refs[9:]
    width = t_ref.shape[-1]

    @pl.when(pl.program_id(0) == 0)
    def _():
        for n, (array, part, _) in enumerate(RING):
            for k in range(CK):
                high, low = split(v_refs[array][part, k])
                v_high[n * AB : (n + 1) * AB, k * width : (k + 1) * width] = high
                v_low[n * AB : (n + 1) * AB, k * width : (k + 1) * width] = low

    total = jnp.zeros((Z * YL * AB, ROWS), jnp.float32)
    dims = (((1,), (1,)), ((), ()))
    for k in range(0, CK, 2):
        rows = jnp.concatenate([t_ref[0, :, k + n].reshape(ROWS, width) for n in range(2)], axis=1)
        high, low = split(rows)
        at = slice(k * width, (k + 2) * width)
        for left, right in ((v_high, high), (v_high, low), (v_low, high)):
            total += lax.dot_general(left[:, at], right, dims, preferred_element_type=jnp.float32)

    labels = labels_ref[0]
    z = lax.axis_index("z")
    for n, (_, part, behind) in enumerate(RING):
        source = YL * lax.rem(z - behind + Z, Z) + (n - len(RING) + YL if behind == 4 else part)
        for g in range(AB // 16):
            tb = (AB * lax.rem(source, Z * YL // SA) + 16 * g) // VT
            at = n * AB + 16 * g
            kept = jnp.where(labels == (vir[0] ^ vir[tb]), total[at : at + 16], 0.0)
            out_ref[0, source, 16 * g : 16 * (g + 1), :] = kept


def contract(received, ring, labels, vir_irrep):
    width = received.shape[-1]
    whole = pl.BlockSpec(memory_space=pltpu.VMEM)
    depth = CK * width
    return pl.pallas_call(
        contract_kernel,
        out_shape=jax.ShapeDtypeStruct((YL, JA, AB, ROWS), jnp.float32),
        grid=(YL,),
        in_specs=[
            pl.BlockSpec(memory_space=pltpu.SMEM),
            pl.BlockSpec((1, 1, ROWS), lambda s: (s, 0, 0)),
            pl.BlockSpec((1, JA, CK, PAIRS, width), lambda s: (s, 0, 0, 0, 0)),
        ]
        + [whole] * len(ring),
        out_specs=pl.BlockSpec((1, JA, AB, ROWS), lambda s: (s, 0, 0, 0)),
        scratch_shapes=[pltpu.VMEM((Z * YL * AB, depth), jnp.bfloat16)] * 2,
        compiler_params=pltpu.CompilerParams(vmem_limit_bytes=VMEM_LIMIT),
        cost_estimate=pl.CostEstimate(flops=6 * 768 * 512 * depth, bytes_accessed=10**7, transcendentals=0),
    )(vir_irrep, labels, received, *ring)


def ladder_parts(tiles, amplitudes, integrals, labels, occ_irrep, vir_irrep):
    forward = [(n, (n + 1) % Z) for n in range(Z)]
    backward = [(n, (n - 1) % Z) for n in range(Z)]
    own = lax.all_to_all(pack_integrals(integrals, vir_irrep, tiles), "yl", split_axis=0, concat_axis=0, tiled=True)
    ring = [own]
    ahead = behind = own
    for _ in range(3):
        behind = lax.ppermute(behind, "z", forward)
        ahead = lax.ppermute(ahead, "z", backward)
        ring += [behind, ahead]
    ring += [lax.ppermute(behind[:1], "z", forward), lax.ppermute(ahead[1:], "z", backward)]
    packed = pack_amplitudes(amplitudes, occ_irrep, vir_irrep, tiles)
    received = lax.all_to_all(
        packed.reshape((YL * JA,) + packed.shape[2:]), ("yl", "ja"), split_axis=0, concat_axis=0, tiled=True
    ).reshape(packed.shape)
    return contract(received, ring, labels, vir_irrep)


def reduce_kernel(parts_ref, out_ref):
    total = parts_ref[0]
    for n in range(1, YL * JA):
        total += parts_ref[n]
    padded = jnp.concatenate([total, jnp.zeros((LANES - AB, ROWS), jnp.float32)], axis=0)
    out_ref[...] = padded.T


def reduce_parts(parts):
    return pl.pallas_call(
        reduce_kernel,
        out_shape=jax.ShapeDtypeStruct((ROWS, LANES), jnp.float32),
        in_specs=[pl.BlockSpec(memory_space=pltpu.VMEM)],
        out_specs=pl.BlockSpec(memory_space=pltpu.VMEM),
        compiler_params=pltpu.CompilerParams(vmem_limit_bytes=VMEM_LIMIT),
    )(parts)


def local(amplitudes, integrals, occ_irrep, vir_irrep, occ_energy, vir_energy):
    z, yl, ja = lax.axis_index("z"), lax.axis_index("yl"), lax.axis_index("ja")
    occ_rows = lax.dynamic_slice_in_dim(occ_irrep, YL * NI * z, YL * NI).reshape(YL, 1, NI, 1)
    labels = jnp.bitwise_xor(occ_rows, occ_irrep.reshape(1, JA, 1, NI)).reshape(YL, 1, ROWS)
    largest = jnp.max(jnp.sum((vir_irrep[:, None] == vir_irrep[None, :]).astype(jnp.int32), axis=1))
    tier = jnp.where(largest <= 2, 0, jnp.where(largest <= 4, 1, 2))
    branches = [functools.partial(ladder_parts, tiles) for tiles in (1, 2, 3)]
    parts = lax.switch(tier, branches, amplitudes, integrals, labels, occ_irrep, vir_irrep)
    parts = lax.all_to_all(
        parts.reshape(YL * JA, AB, ROWS), ("yl", "ja"), split_axis=0, concat_axis=0, tiled=True
    )
    ladder = reduce_parts(parts).reshape(JA, PAIRS, LANES)
    mirror = lax.all_to_all(ladder, ("z", "yl"), split_axis=0, concat_axis=0, tiled=True)
    ladder = ladder.reshape(JA, NI, NI, LANES)[..., :AB].transpose(1, 0, 2, 3).reshape(NI, O, AB)
    mirror = mirror.reshape(JA, NI, NI, LANES)[..., :AB].transpose(2, 0, 1, 3).reshape(NI, O, AB)
    ab_energy = (vir_energy[:SA, None] + vir_energy[None, :]).reshape(SA * NV)
    ab_part = lax.dynamic_slice_in_dim(ab_energy, ja * AB, AB)
    occ_part = lax.dynamic_slice_in_dim(occ_energy, NI * (YL * z + yl), NI)
    denominator = occ_part[:, None, None] + occ_energy[None, :, None] - ab_part[None, None, :]
    return (ladder - mirror) / denominator


def solution(mesh):
    parts = Mesh(mesh.devices.reshape(Z, YL, JA), ("z", "yl", "ja"))
    rows = ("z", "yl")
    in_specs = (P(rows, "ja", None, None), P(rows, "ja", None), P(), P(), P(), P())
    return jax.shard_map(local, mesh=parts, in_specs=in_specs, out_specs=P(rows, None, "ja"), check_vma=False)
```

```python
import functools

import jax
import jax.numpy as jnp
from jax import lax
from jax.experimental import pallas as pl
from jax.experimental.pallas import tpu as pltpu
from jax.sharding import Mesh, PartitionSpec as P

O = 64
NV = 384
VT = 64
SA = 2
NVT = NV // VT
Z = 8
YL = 2
JA = 16
NI = 4
PAIRS = NI * NI
CB = NV // JA
CK = CB // YL
AB = SA * NV // (Z * YL)
ROWS = JA * PAIRS
GROUP = 4
LANES = 128
MIB = 1024 * 1024
KEPT = 64


def layout(slots):
    return [(2 * t, 2 * t + 1) for t in range(slots // 2)] + [(slots - 1, slots - 1)] * (slots % 2)


def lane_tiles(slots):
    return CK * slots // 2


def slot_tiles(wanted, vir, slots):
    lane = lax.broadcasted_iota(jnp.int32, wanted.shape, wanted.ndim - 1)
    slot = jnp.where(lane < VT, slots[0], slots[1])
    count = jnp.zeros(wanted.shape, jnp.int32)
    chosen = jnp.full(wanted.shape, -1, jnp.int32)
    for td in range(NVT):
        match = wanted == vir[td]
        chosen = jnp.where(match & (count == slot), td, chosen)
        count = jnp.where(match, count + 1, count)
    return chosen


def straight_and_turned(chosen):
    half = (lax.broadcasted_iota(jnp.int32, chosen.shape, chosen.ndim - 1) >= VT).astype(jnp.int32)
    return [
        jnp.where((each >= 0) & ((each & 1) == half), each >> 1, -1)
        for each in (chosen, pltpu.roll(chosen, VT, chosen.ndim - 1))
    ]


def pack_tiles(block, chosen_of):
    packed = {}
    for key, chosen in chosen_of.items():
        terms = []
        for each in chosen:
            term = jnp.zeros(block.shape[:2] + (LANES,), jnp.float32)
            for k in range(NV // LANES):
                term = jnp.where(each == k, block[:, :, k * LANES : (k + 1) * LANES], term)
            terms.append(term)
        packed[key] = terms[0] + pltpu.roll(terms[1], VT, 2)
    return packed


def store_tiles(slots, rows, b, packed, out_ref):
    full = slots // 2
    depth = lane_tiles(slots)
    low = lax.broadcasted_iota(jnp.int32, (8, LANES), 1) < VT
    for n in range(rows):
        for t, key in enumerate(layout(slots)):
            values = packed[key][n]
            if t < full:
                for c, count in ((8, 4), (12, 4)) if b == 1 else ((8 * b, 8),):
                    first = ((c // CK) * depth + (c % CK) * full + t) * rows + n
                    out_ref[pl.ds(first, count, stride=full * rows), :] = values[c % 8 : c % 8 + count]
            else:
                values = jnp.where(low, values, pltpu.roll(values, 6, 0))
                for q in range(2):
                    c = 8 * b + 4 * q
                    first = ((c // CK) * depth + CK * full + (c % CK) // 2) * rows + n
                    out_ref[pl.ds(first, 2, stride=rows), :] = values[4 * q : 4 * q + 2]


def pack_amplitudes_kernel(slots, occ, vir, t_ref, out_ref, chosen_ref):
    step = pl.program_id(0)
    keys = layout(slots)

    @pl.when(step == 0)
    def _():
        first_i = NI * (YL * lax.axis_index("z") + lax.axis_index("yl"))
        first_j = NI * lax.axis_index("ja")

        @pl.loop(0, PAIRS)
        def _(p):
            label = occ[first_i + p // NI] ^ occ[first_j + p % NI]
            for tc in range(NVT):
                wanted = jnp.full((8, LANES), label ^ vir[tc], jnp.int32)
                for n, key in enumerate(keys):
                    chosen_ref[tc, n, 0, p], chosen_ref[tc, n, 1, p] = straight_and_turned(slot_tiles(wanted, vir, key))

    @pl.loop(0, GROUP)
    def _(g):
        for b in range(CB // 8):
            tc = ((step * GROUP + g) * (CB // 8) + b) // (VT // 8)
            chosen_of = {key: (chosen_ref[tc, n, 0], chosen_ref[tc, n, 1]) for n, key in enumerate(keys)}
            packed = pack_tiles(t_ref[:, pl.ds(pl.multiple_of(g * CB + b * 8, 8), 8), :], chosen_of)
            store_tiles(slots, PAIRS, b, packed, out_ref.at[g])


def pack_amplitudes(amplitudes, occ_irrep, vir_irrep, slots):
    rows = YL * lane_tiles(slots) * PAIRS
    return pl.pallas_call(
        functools.partial(pack_amplitudes_kernel, slots),
        out_shape=jax.ShapeDtypeStruct((JA, rows, LANES), jnp.float32),
        grid=(JA // GROUP,),
        in_specs=[
            pl.BlockSpec(memory_space=pltpu.SMEM),
            pl.BlockSpec(memory_space=pltpu.SMEM),
            pl.BlockSpec((PAIRS, GROUP * CB, NV), lambda s: (0, s, 0)),
        ],
        out_specs=pl.BlockSpec((GROUP, rows, LANES), lambda s: (s, 0, 0)),
        scratch_shapes=[pltpu.VMEM((NVT, len(layout(slots)), 2, PAIRS, 8, LANES), jnp.int32)],
        compiler_params=pltpu.CompilerParams(vmem_limit_bytes=20 * MIB),
        cost_estimate=pl.CostEstimate(flops=10**7, bytes_accessed=14 * 10**6, transcendentals=0),
    )(occ_irrep, vir_irrep, amplitudes.reshape(PAIRS, NV, NV))


def pack_integrals_kernel(slots, vir, v_ref, kept_ref, sent_ref, packed_ref):
    ia = YL * lax.axis_index("z") + lax.axis_index("yl")
    tb = (AB * (ia % (Z * YL // SA)) + 16 * pl.program_id(0)) // VT
    for b in range(CB // 8):
        tc = (lax.axis_index("ja") * (CB // 8) + b) // (VT // 8)
        wanted = jnp.full((8, LANES), vir[0] ^ vir[tb] ^ vir[tc], jnp.int32)
        chosen_of = {key: straight_and_turned(slot_tiles(wanted, vir, key)) for key in layout(slots)}
        store_tiles(slots, 16, b, pack_tiles(v_ref[:, b * 8 : (b + 1) * 8, :], chosen_of), packed_ref)
    depth = lane_tiles(slots) * 16
    for yl, ref in ((lax.axis_index("yl"), kept_ref), (1 - lax.axis_index("yl"), sent_ref)):
        ref[...] = packed_ref[pl.ds(pl.multiple_of(yl * depth, 16), depth), :].reshape(ref.shape)


def pack_integrals(integrals, vir_irrep, slots):
    depth = lane_tiles(slots)
    return pl.pallas_call(
        functools.partial(pack_integrals_kernel, slots),
        out_shape=[jax.ShapeDtypeStruct((depth, AB, LANES), jnp.float32)] * 2,
        grid=(AB // 16,),
        in_specs=[
            pl.BlockSpec(memory_space=pltpu.SMEM),
            pl.BlockSpec((16, CB, NV), lambda s: (s, 0, 0)),
        ],
        out_specs=[pl.BlockSpec((depth, 16, LANES), lambda s: (0, s, 0))] * 2,
        scratch_shapes=[pltpu.VMEM((YL * depth * 16, LANES), jnp.float32)],
        compiler_params=pltpu.CompilerParams(vmem_limit_bytes=12 * MIB),
        cost_estimate=pl.CostEstimate(flops=10**6, bytes_accessed=3 * 10**6, transcendentals=0),
    )(vir_irrep, integrals)


def split(values):
    high = values.astype(jnp.bfloat16)
    return high, (values - high.astype(jnp.float32)).astype(jnp.bfloat16)


def dot(left, right, right_dim):
    return lax.dot_general(left, right, (((1,), (right_dim,)), ((), ())), preferred_element_type=jnp.float32)


def place(values, chosen, right_dim):
    terms = dot(jnp.concatenate(split(values), axis=0), chosen, right_dim)
    return terms[: values.shape[0]] + terms[values.shape[0] :]


def kept_rows(labels, wanted):
    at = lax.broadcasted_iota(jnp.int32, (8, ROWS), 0)
    label_of = jnp.zeros((8, ROWS), jnp.int32)
    for n, label in enumerate(wanted):
        label_of = jnp.where(at == n, label, label_of)
    match = (label_of == labels) & (at < len(wanted))
    before = lax.broadcasted_iota(jnp.int32, (ROWS, ROWS), 0) < lax.broadcasted_iota(jnp.int32, (ROWS, ROWS), 1)
    rank = dot(jnp.where(match, 1.0, 0.0).astype(jnp.bfloat16), jnp.where(before, 1.0, 0.0).astype(jnp.bfloat16), 0)
    rank = jnp.where(match, rank.astype(jnp.int32), -ROWS)
    slot = lax.broadcasted_iota(jnp.int32, (LANES, ROWS), 0)
    return [
        [jnp.where(rank[n : n + 1] + shift == slot, 1.0, 0.0).astype(jnp.bfloat16) for shift in (0, KEPT)]
        for n in range(len(wanted))
    ]


HOPS = [(other, side * n) for n in range(1, 4) for other in range(YL) for side in (1, -1)] + [(0, 4), (1, -4)]
RING = sorted([(0, 0), (1, 0)] + HOPS, key=lambda of: (of[1] % Z, of[0]))
BLOCKS = SA * NV // 16
TILE_BLOCKS = VT // 16


def contract_kernel(keep_all, vir, labels_ref, t_ref, *refs):
    v_refs, (out_ref, v_held, sem, v_high, v_low, t_high, t_low, sums_ref) = refs[: len(RING)], refs[len(RING) :]
    depth = t_ref.shape[2]

    copies = [pltpu.make_async_copy(v_ref, v_held.at[n], sem.at[n]) for n, v_ref in enumerate(v_refs)]

    @pl.when(pl.program_id(0) == 0)
    def _():
        for copy in copies:
            copy.start()

    @pl.loop(0, depth)
    def _(k):
        at = pl.ds(pl.multiple_of(k * LANES, LANES), LANES)
        t_high[:, at], t_low[:, at] = split(t_ref[:, 0, k].reshape(ROWS, LANES))

    @pl.when(pl.program_id(0) == 0)
    def _():
        for copy in copies:
            copy.wait()

        @pl.loop(0, depth)
        def _(k):
            at = pl.ds(pl.multiple_of(k * LANES, LANES), LANES)
            v_high[:, at], v_low[:, at] = split(v_held[:, k].reshape(SA * NV, LANES))

    @pl.loop(0, 3)
    def _(m):
        at = pl.ds(pl.multiple_of(m * 256, 256), 256)
        high, low = v_high[at], v_low[at]
        total = dot(high, t_high[...], 1) + dot(high, t_low[...], 1) + dot(low, t_high[...], 1)
        sums_ref[pl.ds(m * 16, 16)] = total.reshape(16, 16, ROWS)

    z, yl = lax.axis_index("z"), lax.axis_index("yl")

    def sums_at(block):
        source = block // 3
        return 3 * (YL * lax.rem(z - source // YL + Z, Z) + (yl ^ (source % YL))) + block % 3

    labels = labels_ref[0]
    wanted = [vir[0] ^ vir[tb] for tb in range(NVT)]
    if keep_all:
        for n in range(BLOCKS):
            kept = jnp.where(labels == wanted[n % (BLOCKS // SA) // TILE_BLOCKS], sums_ref[sums_at(n)], 0.0)
            out_ref[0, n // 3, 16 * (n % 3) : 16 * (n % 3) + 16, :] = kept
        return
    for tb, (first, second) in enumerate(kept_rows(labels, wanted)):
        blocks = [a * (BLOCKS // SA) + tb * TILE_BLOCKS + q for a in range(SA) for q in range(TILE_BLOCKS)]
        upper = jnp.concatenate([sums_ref[sums_at(n), :8] for n in blocks], axis=0)
        lower = jnp.concatenate([sums_ref[sums_at(n), 8:] for n in blocks], axis=0)
        kept = place(upper, first, 1) + place(lower, second, 1)
        for m, n in enumerate(blocks):
            out_ref[0, n // 3, 8 * (n % 3) : 8 * (n % 3) + 8, :] = kept[8 * m : 8 * m + 8]


def contract(received, ring, labels, vir_irrep, slots, keep_all):
    depth = lane_tiles(slots)
    rest = (AB, ROWS) if keep_all else (AB // 2, LANES)
    return pl.pallas_call(
        functools.partial(contract_kernel, keep_all),
        out_shape=jax.ShapeDtypeStruct((YL, JA) + rest, jnp.float32),
        grid=(YL,),
        in_specs=[
            pl.BlockSpec(memory_space=pltpu.SMEM),
            pl.BlockSpec((1, 1, ROWS), lambda s: (s, 0, 0)),
            pl.BlockSpec((JA, 1, depth, PAIRS, LANES), lambda s: (0, s, 0, 0, 0)),
        ]
        + [pl.BlockSpec(memory_space=pl.ANY)] * len(ring),
        out_specs=pl.BlockSpec((1, JA) + rest, lambda s: (s, 0, 0, 0)),
        scratch_shapes=[pltpu.VMEM((Z * YL, depth, AB, LANES), jnp.float32), pltpu.SemaphoreType.DMA((Z * YL,))]
        + [pltpu.VMEM((Z * YL * AB, depth * LANES), jnp.bfloat16)] * 2
        + [pltpu.VMEM((ROWS, depth * LANES), jnp.bfloat16)] * 2
        + [pltpu.VMEM((BLOCKS, 16, ROWS), jnp.float32)],
        compiler_params=pltpu.CompilerParams(vmem_limit_bytes=60 * MIB),
        cost_estimate=pl.CostEstimate(flops=6 * 768 * 512 * LANES * depth, bytes_accessed=10**7, transcendentals=0),
    )(vir_irrep, labels, received, *ring)


def reduce_kernel(keep_all, vir, labels_ref, parts_ref, out_ref):
    total = parts_ref[0]
    for n in range(1, YL * JA):
        total += parts_ref[n]
    if keep_all:
        rows = [total]
    else:
        first_block = lax.axis_index("ja") * (AB // 16)
        wanted = [vir[0] ^ vir[(first_block + g) % (BLOCKS // SA) // TILE_BLOCKS] for g in range(AB // 16)]
        rows = []
        for g, chosen in enumerate(kept_rows(labels_ref[lax.axis_index("yl")], wanted)):
            rows += [place(total[8 * g : 8 * g + 8], each, 0) for each in chosen]
    out_ref[...] = jnp.concatenate(rows + [jnp.zeros((LANES - AB, ROWS), jnp.float32)], axis=0).T


def reduce_parts(parts, labels, vir_irrep, keep_all):
    whole = pl.BlockSpec(memory_space=pltpu.VMEM)
    return pl.pallas_call(
        functools.partial(reduce_kernel, keep_all),
        out_shape=jax.ShapeDtypeStruct((ROWS, LANES), jnp.float32),
        in_specs=[pl.BlockSpec(memory_space=pltpu.SMEM), whole, whole],
        out_specs=whole,
        compiler_params=pltpu.CompilerParams(vmem_limit_bytes=12 * MIB),
    )(vir_irrep, labels, parts)


def finish(ladder, occ_energy, vir_energy):
    z, yl, ja = lax.axis_index("z"), lax.axis_index("yl"), lax.axis_index("ja")
    mirror = lax.all_to_all(ladder, ("z", "yl"), split_axis=0, concat_axis=0, tiled=True)
    ladder = ladder.reshape(JA, NI, NI, LANES)[..., :AB].transpose(1, 0, 2, 3).reshape(NI, O, AB)
    mirror = mirror.reshape(JA, NI, NI, LANES)[..., :AB].transpose(2, 0, 1, 3).reshape(NI, O, AB)
    ab_energy = (vir_energy[:SA, None] + vir_energy[None, :]).reshape(SA * NV)
    ab_part = lax.dynamic_slice_in_dim(ab_energy, ja * AB, AB)
    occ_part = lax.dynamic_slice_in_dim(occ_energy, NI * (YL * z + yl), NI)
    denominator = occ_part[:, None, None] + occ_energy[None, :, None] - ab_part[None, None, :]
    return (ladder - mirror) / denominator


def residual_rows(slots, keep_all, amplitudes, integrals, occ_irrep, vir_irrep, occ_energy, vir_energy):
    forward = [(n, (n + 1) % Z) for n in range(Z)]
    backward = [(n, (n - 1) % Z) for n in range(Z)]
    kept, sent = pack_integrals(integrals, vir_irrep, slots)
    neighbours = lax.ppermute(sent, "yl", [(0, 1), (1, 0)])
    ring = {(0, 0): kept, (1, 0): neighbours}

    def hop(other, behind):
        side = 1 if behind > 0 else -1
        ring[other, behind] = lax.ppermute(ring[other, behind - side], "z", forward if side > 0 else backward)

    for of in HOPS[:4]:
        hop(*of)
    packed = pack_amplitudes(amplitudes, occ_irrep, vir_irrep, slots)
    packed, *first = lax.optimization_barrier((packed, *(ring[of] for of in HOPS[:4])))
    ring |= dict(zip(HOPS[:4], first))
    for of in HOPS[4:]:
        hop(*of)
    ring = [ring[key] for key in RING]
    received = lax.all_to_all(
        packed.reshape(JA * YL, lane_tiles(slots) * PAIRS, LANES), ("ja", "yl"), split_axis=0, concat_axis=0, tiled=True
    ).reshape(JA, YL, lane_tiles(slots), PAIRS, LANES)
    occ_rows = lax.dynamic_slice_in_dim(occ_irrep, YL * NI * lax.axis_index("z"), YL * NI).reshape(YL, 1, NI, 1)
    labels = jnp.bitwise_xor(occ_rows, occ_irrep.reshape(1, JA, 1, NI)).reshape(YL, 1, ROWS)
    parts = contract(received, ring, labels, vir_irrep, slots, keep_all)
    parts = lax.all_to_all(
        parts.reshape((YL * JA,) + parts.shape[2:]), ("yl", "ja"), split_axis=0, concat_axis=0, tiled=True
    )
    ladder = reduce_parts(parts, labels, vir_irrep, keep_all).reshape(JA, PAIRS, LANES)
    return finish(ladder, occ_energy, vir_energy)


def largest_class(labels):
    counts = jnp.sum((labels[:, None] == jnp.arange(8)[None, :]).astype(jnp.int32), axis=0)
    return jnp.max(counts)


def local(amplitudes, integrals, occ_irrep, vir_irrep, occ_energy, vir_energy):
    tier = jnp.maximum(jnp.where(largest_class(vir_irrep) > 2, 1, 0), jnp.where(largest_class(occ_irrep) > KEPT // NI, 1, 0))
    branches = [functools.partial(residual_rows, *of) for of in ((2, False), (NVT, True))]
    return lax.switch(tier, branches, amplitudes, integrals, occ_irrep, vir_irrep, occ_energy, vir_energy)


def solution(mesh):
    parts = Mesh(mesh.devices.reshape(Z, YL, JA), ("z", "yl", "ja"))
    rows = ("z", "yl")
    in_specs = (P(rows, "ja", None, None), P(rows, "ja", None), P(), P(), P(), P())
    return jax.shard_map(local, mesh=parts, in_specs=in_specs, out_specs=P(rows, None, "ja"), check_vma=False)
```

```python
import functools

import jax
import jax.numpy as jnp
from jax import lax
from jax.experimental import pallas as pl
from jax.experimental.pallas import tpu as pltpu
from jax.sharding import Mesh, PartitionSpec as P

O = 64
NV = 384
VT = 64
SA = 2
NVT = NV // VT
Z = 8
YL = 2
JA = 16
NI = 4
PAIRS = NI * NI
CB = NV // JA
CK = CB // YL
AB = SA * NV // (Z * YL)
ROWS = JA * PAIRS
GROUP = 4
LANES = 128
MIB = 1024 * 1024
KEPT = 64


def layout(slots):
    return [(2 * t, 2 * t + 1) for t in range(slots // 2)] + [(slots - 1, slots - 1)] * (slots % 2)


def lane_tiles(slots):
    return CK * slots // 2


def slot_tiles(wanted, vir, slots):
    lane = lax.broadcasted_iota(jnp.int32, wanted.shape, wanted.ndim - 1)
    slot = jnp.where(lane < VT, slots[0], slots[1])
    count = jnp.zeros(wanted.shape, jnp.int32)
    chosen = jnp.full(wanted.shape, -1, jnp.int32)
    for td in range(NVT):
        match = wanted == vir[td]
        chosen = jnp.where(match & (count == slot), td, chosen)
        count = jnp.where(match, count + 1, count)
    return chosen


def straight_and_turned(chosen):
    half = (lax.broadcasted_iota(jnp.int32, chosen.shape, chosen.ndim - 1) >= VT).astype(jnp.int32)
    return [
        jnp.where((each >= 0) & ((each & 1) == half), each >> 1, -1)
        for each in (chosen, pltpu.roll(chosen, VT, chosen.ndim - 1))
    ]


def pack_tiles(block, chosen_of):
    packed = {}
    for key, chosen in chosen_of.items():
        terms = []
        for each in chosen:
            term = jnp.zeros(block.shape[:2] + (LANES,), jnp.float32)
            for k in range(NV // LANES):
                term = jnp.where(each == k, block[:, :, k * LANES : (k + 1) * LANES], term)
            terms.append(term)
        packed[key] = terms[0] + pltpu.roll(terms[1], VT, 2)
    return packed


def store_tiles(slots, rows, b, packed, out_ref):
    full = slots // 2
    depth = lane_tiles(slots)
    low = lax.broadcasted_iota(jnp.int32, (8, LANES), 1) < VT
    for n in range(rows):
        for t, key in enumerate(layout(slots)):
            values = packed[key][n]
            if t < full:
                for c, count in ((8, 4), (12, 4)) if b == 1 else ((8 * b, 8),):
                    first = ((c // CK) * depth + (c % CK) * full + t) * rows + n
                    out_ref[pl.ds(first, count, stride=full * rows), :] = values[c % 8 : c % 8 + count]
            else:
                values = jnp.where(low, values, pltpu.roll(values, 6, 0))
                for q in range(2):
                    c = 8 * b + 4 * q
                    first = ((c // CK) * depth + CK * full + (c % CK) // 2) * rows + n
                    out_ref[pl.ds(first, 2, stride=rows), :] = values[4 * q : 4 * q + 2]


def pack_amplitudes_kernel(slots, occ, vir, t_ref, out_ref, chosen_ref):
    step = pl.program_id(0)
    keys = layout(slots)

    @pl.when(step == 0)
    def _():
        first_i = NI * (YL * lax.axis_index("z") + lax.axis_index("yl"))
        first_j = NI * lax.axis_index("ja")

        @pl.loop(0, PAIRS)
        def _(p):
            label = occ[first_i + p // NI] ^ occ[first_j + p % NI]
            for tc in range(NVT):
                wanted = jnp.full((8, LANES), label ^ vir[tc], jnp.int32)
                for n, key in enumerate(keys):
                    chosen_ref[tc, n, 0, p], chosen_ref[tc, n, 1, p] = straight_and_turned(slot_tiles(wanted, vir, key))

    @pl.loop(0, GROUP)
    def _(g):
        for b in range(CB // 8):
            tc = ((step * GROUP + g) * (CB // 8) + b) // (VT // 8)
            chosen_of = {key: (chosen_ref[tc, n, 0], chosen_ref[tc, n, 1]) for n, key in enumerate(keys)}
            packed = pack_tiles(t_ref[:, pl.ds(pl.multiple_of(g * CB + b * 8, 8), 8), :], chosen_of)
            store_tiles(slots, PAIRS, b, packed, out_ref.at[g])


def pack_amplitudes(amplitudes, occ_irrep, vir_irrep, slots):
    rows = YL * lane_tiles(slots) * PAIRS
    return pl.pallas_call(
        functools.partial(pack_amplitudes_kernel, slots),
        out_shape=jax.ShapeDtypeStruct((JA, rows, LANES), jnp.float32),
        grid=(JA // GROUP,),
        in_specs=[
            pl.BlockSpec(memory_space=pltpu.SMEM),
            pl.BlockSpec(memory_space=pltpu.SMEM),
            pl.BlockSpec((PAIRS, GROUP * CB, NV), lambda s: (0, s, 0)),
        ],
        out_specs=pl.BlockSpec((GROUP, rows, LANES), lambda s: (s, 0, 0)),
        scratch_shapes=[pltpu.VMEM((NVT, len(layout(slots)), 2, PAIRS, 8, LANES), jnp.int32)],
        compiler_params=pltpu.CompilerParams(vmem_limit_bytes=20 * MIB),
        cost_estimate=pl.CostEstimate(flops=10**7, bytes_accessed=14 * 10**6, transcendentals=0),
    )(occ_irrep, vir_irrep, amplitudes.reshape(PAIRS, NV, NV))


def pack_integrals_kernel(slots, vir, v_ref, kept_ref, sent_ref, packed_ref):
    ia = YL * lax.axis_index("z") + lax.axis_index("yl")
    tb = (AB * (ia % (Z * YL // SA)) + 16 * pl.program_id(0)) // VT
    for b in range(CB // 8):
        tc = (lax.axis_index("ja") * (CB // 8) + b) // (VT // 8)
        wanted = jnp.full((8, LANES), vir[0] ^ vir[tb] ^ vir[tc], jnp.int32)
        chosen_of = {key: straight_and_turned(slot_tiles(wanted, vir, key)) for key in layout(slots)}
        store_tiles(slots, 16, b, pack_tiles(v_ref[:, b * 8 : (b + 1) * 8, :], chosen_of), packed_ref)
    depth = lane_tiles(slots) * 16
    for yl, ref in ((lax.axis_index("yl"), kept_ref), (1 - lax.axis_index("yl"), sent_ref)):
        ref[...] = packed_ref[pl.ds(pl.multiple_of(yl * depth, 16), depth), :].reshape(ref.shape)


def pack_integrals(integrals, vir_irrep, slots):
    depth = lane_tiles(slots)
    return pl.pallas_call(
        functools.partial(pack_integrals_kernel, slots),
        out_shape=[jax.ShapeDtypeStruct((depth, AB, LANES), jnp.float32)] * 2,
        grid=(AB // 16,),
        in_specs=[
            pl.BlockSpec(memory_space=pltpu.SMEM),
            pl.BlockSpec((16, CB, NV), lambda s: (s, 0, 0)),
        ],
        out_specs=[pl.BlockSpec((depth, 16, LANES), lambda s: (0, s, 0))] * 2,
        scratch_shapes=[pltpu.VMEM((YL * depth * 16, LANES), jnp.float32)],
        compiler_params=pltpu.CompilerParams(vmem_limit_bytes=12 * MIB),
        cost_estimate=pl.CostEstimate(flops=10**6, bytes_accessed=3 * 10**6, transcendentals=0),
    )(vir_irrep, integrals)


def split(values):
    high = values.astype(jnp.bfloat16)
    return high, (values - high.astype(jnp.float32)).astype(jnp.bfloat16)


def dot(left, right, right_dim):
    return lax.dot_general(left, right, (((1,), (right_dim,)), ((), ())), preferred_element_type=jnp.float32)


def place(values, chosen, right_dim):
    terms = dot(jnp.concatenate(split(values), axis=0), chosen, right_dim)
    return terms[: values.shape[0]] + terms[values.shape[0] :]


def kept_rows(labels, wanted):
    at = lax.broadcasted_iota(jnp.int32, (8, ROWS), 0)
    label_of = jnp.zeros((8, ROWS), jnp.int32)
    for n, label in enumerate(wanted):
        label_of = jnp.where(at == n, label, label_of)
    match = (label_of == labels) & (at < len(wanted))
    before = lax.broadcasted_iota(jnp.int32, (ROWS, ROWS), 0) < lax.broadcasted_iota(jnp.int32, (ROWS, ROWS), 1)
    rank = dot(jnp.where(match, 1.0, 0.0).astype(jnp.bfloat16), jnp.where(before, 1.0, 0.0).astype(jnp.bfloat16), 0)
    rank = jnp.where(match, rank.astype(jnp.int32), -ROWS)
    slot = lax.broadcasted_iota(jnp.int32, (LANES, ROWS), 0)
    return [
        [jnp.where(rank[n : n + 1] + shift == slot, 1.0, 0.0).astype(jnp.bfloat16) for shift in (0, KEPT)]
        for n in range(len(wanted))
    ]


HOPS = [(other, side * n) for n in range(1, 4) for other in range(YL) for side in (1, -1)] + [(0, 4), (1, -4)]
RING = sorted([(0, 0), (1, 0)] + HOPS, key=lambda of: (of[1] % Z, of[0]))
BLOCKS = SA * NV // 16
TILE_BLOCKS = VT // 16


def contract_kernel(keep_all, vir, labels_ref, t_ref, *refs):
    v_refs, (out_ref, v_held, sem, v_high, v_low, t_high, t_low, sums_ref, kept_ref) = refs[:-9], refs[-9:]
    depth = t_ref.shape[2]

    copies, first = [], 0
    for v_ref in v_refs:
        copies.append(pltpu.make_async_copy(v_ref, v_held.at[pl.ds(first, v_ref.shape[0])], sem.at[first]))
        first += v_ref.shape[0]

    @pl.when(pl.program_id(0) == 0)
    def _():
        for copy in copies:
            copy.start()

    labels = labels_ref[0]
    wanted = [vir[0] ^ vir[tb] for tb in range(NVT)]
    if not keep_all:
        for tb, matrices in enumerate(kept_rows(labels, wanted)):
            for n, matrix in enumerate(matrices):
                kept_ref[tb, :, n * ROWS : (n + 1) * ROWS] = matrix

    @pl.loop(0, depth)
    def _(k):
        at = pl.ds(pl.multiple_of(k * LANES, LANES), LANES)
        t_high[:, at], t_low[:, at] = split(t_ref[:, 0, k].reshape(ROWS, LANES))

    @pl.when(pl.program_id(0) == 0)
    def _():
        for copy in copies:
            copy.wait()

        @pl.loop(0, depth)
        def _(k):
            at = pl.ds(pl.multiple_of(k * LANES, LANES), LANES)
            v_high[:, at], v_low[:, at] = split(v_held[:, k].reshape(SA * NV, LANES))

    part = 384

    @pl.loop(0, SA * NV // part)
    def _(m):
        at = pl.ds(pl.multiple_of(m * part, part), part)
        high, low = v_high[at], v_low[at]
        total = dot(high, t_high[...], 1) + dot(high, t_low[...], 1) + dot(low, t_high[...], 1)
        sums_ref[pl.ds(m * (part // 16), part // 16)] = total.reshape(part // 16, 16, ROWS)

    z, yl = lax.axis_index("z"), lax.axis_index("yl")

    def sums_at(block):
        source = block // 3
        return 3 * (YL * lax.rem(z - source // YL + Z, Z) + (yl ^ (source % YL))) + block % 3

    if keep_all:
        for n in range(BLOCKS):
            kept = jnp.where(labels == wanted[n % (BLOCKS // SA) // TILE_BLOCKS], sums_ref[sums_at(n)], 0.0)
            out_ref[0, n // 3, 16 * (n % 3) : 16 * (n % 3) + 16, :] = kept
        return
    for tb in range(NVT):
        blocks = [a * (BLOCKS // SA) + tb * TILE_BLOCKS + q for a in range(SA) for q in range(TILE_BLOCKS)]
        sums = [sums_ref[sums_at(n)] for n in blocks]
        sums = jnp.concatenate([jnp.concatenate([each[:8], each[8:]], axis=1) for each in sums], axis=0)
        kept = place(sums, kept_ref[tb], 1)
        for m, n in enumerate(blocks):
            out_ref[0, n // 3, 8 * (n % 3) : 8 * (n % 3) + 8, :] = kept[8 * m : 8 * m + 8]


def contract(received, ring, labels, vir_irrep, slots, keep_all):
    depth = lane_tiles(slots)
    rest = (AB, ROWS) if keep_all else (AB // 2, LANES)
    return pl.pallas_call(
        functools.partial(contract_kernel, keep_all),
        out_shape=jax.ShapeDtypeStruct((YL, JA) + rest, jnp.float32),
        grid=(YL,),
        in_specs=[
            pl.BlockSpec(memory_space=pltpu.SMEM),
            pl.BlockSpec((1, 1, ROWS), lambda s: (s, 0, 0)),
            pl.BlockSpec((JA, 1, depth, PAIRS, LANES), lambda s: (0, s, 0, 0, 0)),
        ]
        + [pl.BlockSpec(memory_space=pl.ANY)] * len(ring),
        out_specs=pl.BlockSpec((1, JA) + rest, lambda s: (s, 0, 0, 0)),
        scratch_shapes=[pltpu.VMEM((Z * YL, depth, AB, LANES), jnp.float32), pltpu.SemaphoreType.DMA((Z * YL,))]
        + [pltpu.VMEM((Z * YL * AB, depth * LANES), jnp.bfloat16)] * 2
        + [pltpu.VMEM((ROWS, depth * LANES), jnp.bfloat16)] * 2
        + [pltpu.VMEM((BLOCKS, 16, ROWS), jnp.float32), pltpu.VMEM((NVT, LANES, 2 * ROWS), jnp.bfloat16)],
        compiler_params=pltpu.CompilerParams(vmem_limit_bytes=60 * MIB),
        cost_estimate=pl.CostEstimate(flops=6 * 768 * 512 * LANES * depth, bytes_accessed=10**7, transcendentals=0),
    )(vir_irrep, labels, received, *ring)


def reduce_kernel(keep_all, vir, labels_ref, parts_ref, out_ref):
    total = parts_ref[0]
    for n in range(1, YL * JA):
        total += parts_ref[n]
    if keep_all:
        rows = [total]
    else:
        first_block = lax.axis_index("ja") * (AB // 16)
        wanted = [vir[0] ^ vir[(first_block + g) % (BLOCKS // SA) // TILE_BLOCKS] for g in range(AB // 16)]
        rows = []
        for g, chosen in enumerate(kept_rows(labels_ref[lax.axis_index("yl")], wanted)):
            rows += [place(total[8 * g : 8 * g + 8], each, 0) for each in chosen]
    out_ref[...] = jnp.concatenate(rows + [jnp.zeros((LANES - AB, ROWS), jnp.float32)], axis=0).T


def reduce_parts(parts, labels, vir_irrep, keep_all):
    whole = pl.BlockSpec(memory_space=pltpu.VMEM)
    return pl.pallas_call(
        functools.partial(reduce_kernel, keep_all),
        out_shape=jax.ShapeDtypeStruct((ROWS, LANES), jnp.float32),
        in_specs=[pl.BlockSpec(memory_space=pltpu.SMEM), whole, whole],
        out_specs=whole,
        compiler_params=pltpu.CompilerParams(vmem_limit_bytes=12 * MIB),
    )(vir_irrep, labels, parts)


def finish(ladder, occ_energy, vir_energy):
    z, yl, ja = lax.axis_index("z"), lax.axis_index("yl"), lax.axis_index("ja")
    mirror = lax.all_to_all(ladder, ("z", "yl"), split_axis=0, concat_axis=0, tiled=True)
    ladder = ladder.reshape(JA, NI, NI, LANES)[..., :AB].transpose(1, 0, 2, 3).reshape(NI, O, AB)
    mirror = mirror.reshape(JA, NI, NI, LANES)[..., :AB].transpose(2, 0, 1, 3).reshape(NI, O, AB)
    ab_energy = (vir_energy[:SA, None] + vir_energy[None, :]).reshape(SA * NV)
    ab_part = lax.dynamic_slice_in_dim(ab_energy, ja * AB, AB)
    occ_part = lax.dynamic_slice_in_dim(occ_energy, NI * (YL * z + yl), NI)
    denominator = occ_part[:, None, None] + occ_energy[None, :, None] - ab_part[None, None, :]
    return (ladder - mirror) / denominator


def ladder_rows(slots, whole, keep_all, amplitudes, integrals, occ_irrep, vir_irrep):
    forward = [(n, (n + 1) % Z) for n in range(Z)]
    backward = [(n, (n - 1) % Z) for n in range(Z)]
    kept, sent = pack_integrals(integrals, vir_irrep, slots)
    neighbours = lax.ppermute(sent, "yl", [(0, 1), (1, 0)])
    if keep_all:
        both, occ_irrep = lax.optimization_barrier((jnp.stack([kept, neighbours]), occ_irrep))
        packed = pack_amplitudes(amplitudes, occ_irrep, vir_irrep, slots)

        def turn(n, carried):
            behind, ahead, blocks = carried
            behind, ahead = lax.ppermute(behind, "z", forward), lax.ppermute(ahead, "z", backward)
            blocks = lax.dynamic_update_index_in_dim(blocks, behind, n, 0)
            return behind, ahead, lax.dynamic_update_index_in_dim(blocks, ahead, Z - n, 0)

        blocks = jnp.broadcast_to(both, (Z,) + both.shape)
        blocks = lax.fori_loop(1, Z // 2 + 1, turn, (both, both, blocks))[2]
        ring = [blocks.reshape((Z * YL,) + kept.shape)]
    elif whole:
        packed = pack_amplitudes(amplitudes, occ_irrep, vir_irrep, slots)
        packed, neighbours = lax.optimization_barrier((packed, neighbours))
        blocks = {0: jnp.stack([kept, neighbours])}
        for n in range(1, Z // 2):
            blocks[n] = lax.ppermute(blocks[n - 1], "z", forward)
            blocks[-n] = lax.ppermute(blocks[1 - n], "z", backward)
        last = [lax.ppermute(blocks[3][:1], "z", forward), lax.ppermute(blocks[-3][1:], "z", backward)]
        ring = [*(blocks[n] for n in range(Z // 2)), *last, *(blocks[n - Z // 2] for n in range(1, Z // 2))]
    else:
        ring = {(0, 0): kept, (1, 0): neighbours}

        def hop(other, behind):
            side = 1 if behind > 0 else -1
            ring[other, behind] = lax.ppermute(ring[other, behind - side], "z", forward if side > 0 else backward)

        for of in HOPS[:2]:
            hop(*of)
        packed = pack_amplitudes(amplitudes, occ_irrep, vir_irrep, slots)
        packed, ring[1, 0], ring[0, 1], ring[0, -1] = lax.optimization_barrier((packed, ring[1, 0], ring[0, 1], ring[0, -1]))
        for of in HOPS[2:]:
            hop(*of)
        ring = [ring[key][None] for key in RING]
    received = lax.all_to_all(
        packed.reshape(JA * YL, lane_tiles(slots) * PAIRS, LANES), ("ja", "yl"), split_axis=0, concat_axis=0, tiled=True
    ).reshape(JA, YL, lane_tiles(slots), PAIRS, LANES)
    occ_rows = lax.dynamic_slice_in_dim(occ_irrep, YL * NI * lax.axis_index("z"), YL * NI).reshape(YL, 1, NI, 1)
    labels = jnp.bitwise_xor(occ_rows, occ_irrep.reshape(1, JA, 1, NI)).reshape(YL, 1, ROWS)
    parts = contract(received, ring, labels, vir_irrep, slots, keep_all)
    parts = lax.all_to_all(
        parts.reshape((YL * JA,) + parts.shape[2:]), ("yl", "ja"), split_axis=0, concat_axis=0, tiled=True
    )
    return reduce_parts(parts, labels, vir_irrep, keep_all)


def tier_kernel(occ, vir, out_ref):
    def largest_class(ref):
        def count(n, counts):
            one = lax.shift_left(1, 8 * (ref[n] & 3))
            return counts[0] + jnp.where(ref[n] < 4, one, 0), counts[1] + jnp.where(ref[n] < 4, 0, one)

        counts = lax.fori_loop(0, ref.shape[0], count, (jnp.int32(0), jnp.int32(0)), unroll=True)
        largest = jnp.int32(0)
        for four in counts:
            for n in range(4):
                largest = jnp.maximum(largest, lax.shift_right_logical(four, 8 * n) & 255)
        return largest

    out_ref[0] = jnp.where(largest_class(occ) <= KEPT // NI, jnp.minimum(jnp.maximum(largest_class(vir) - 2, 0), 2), 2)


def local(amplitudes, integrals, occ_irrep, vir_irrep, occ_energy, vir_energy):
    scalars = pl.BlockSpec(memory_space=pltpu.SMEM)
    tier = pl.pallas_call(
        tier_kernel, out_shape=jax.ShapeDtypeStruct((1,), jnp.int32), in_specs=[scalars] * 2, out_specs=scalars
    )(occ_irrep, vir_irrep)
    branches = [functools.partial(ladder_rows, *of) for of in ((2, False, False), (3, True, False), (NVT, True, True))]
    ladder = lax.switch(tier[0], branches, amplitudes, integrals, occ_irrep, vir_irrep)
    return finish(ladder.reshape(JA, PAIRS, LANES), occ_energy, vir_energy)


def solution(mesh):
    parts = Mesh(mesh.devices.reshape(Z, YL, JA), ("z", "yl", "ja"))
    rows = ("z", "yl")
    in_specs = (P(rows, "ja", None, None), P(rows, "ja", None), P(), P(), P(), P())
    return jax.shard_map(local, mesh=parts, in_specs=in_specs, out_specs=P(rows, None, "ja"), check_vma=False)
```

```python
import functools

import jax
import jax.numpy as jnp
from jax import lax
from jax.experimental import pallas as pl
from jax.experimental.pallas import tpu as pltpu
from jax.sharding import Mesh, PartitionSpec as P

O = 64
NV = 384
VT = 64
SA = 2
NVT = NV // VT
Z = 8
YL = 2
JA = 16
NI = 4
PAIRS = NI * NI
CB = NV // JA
CK = CB // YL
AB = SA * NV // (Z * YL)
ROWS = JA * PAIRS
GROUP = 4
LANES = 128
MIB = 1024 * 1024
KEPT = 64


def layout(slots):
    return [(2 * t, 2 * t + 1) for t in range(slots // 2)] + [(slots - 1, slots - 1)] * (slots % 2)


def lane_tiles(slots):
    return CK * slots // 2


def slot_tiles(wanted, vir, slots):
    lane = lax.broadcasted_iota(jnp.int32, wanted.shape, wanted.ndim - 1)
    slot = jnp.where(lane < VT, slots[0], slots[1])
    count = jnp.zeros(wanted.shape, jnp.int32)
    chosen = jnp.full(wanted.shape, -1, jnp.int32)
    for td in range(NVT):
        match = wanted == vir[td]
        chosen = jnp.where(match & (count == slot), td, chosen)
        count = jnp.where(match, count + 1, count)
    return chosen


def straight_and_turned(chosen):
    half = (lax.broadcasted_iota(jnp.int32, chosen.shape, chosen.ndim - 1) >= VT).astype(jnp.int32)
    return [
        jnp.where((each >= 0) & ((each & 1) == half), each >> 1, -1)
        for each in (chosen, pltpu.roll(chosen, VT, chosen.ndim - 1))
    ]


def pack_tiles(block, chosen_of):
    packed = {}
    for key, chosen in chosen_of.items():
        terms = []
        for each in chosen:
            term = jnp.zeros(block.shape[:2] + (LANES,), jnp.float32)
            for k in range(NV // LANES):
                term = jnp.where(each == k, block[:, :, k * LANES : (k + 1) * LANES], term)
            terms.append(term)
        packed[key] = terms[0] + pltpu.roll(terms[1], VT, 2)
    return packed


def store_tiles(slots, rows, b, packed, out_ref):
    full = slots // 2
    depth = lane_tiles(slots)
    low = lax.broadcasted_iota(jnp.int32, (8, LANES), 1) < VT
    for n in range(rows):
        for t, key in enumerate(layout(slots)):
            values = packed[key][n]
            if t < full:
                for c, count in ((8, 4), (12, 4)) if b == 1 else ((8 * b, 8),):
                    first = ((c // CK) * depth + (c % CK) * full + t) * rows + n
                    out_ref[pl.ds(first, count, stride=full * rows), :] = values[c % 8 : c % 8 + count]
            else:
                values = jnp.where(low, values, pltpu.roll(values, 6, 0))
                for q in range(2):
                    c = 8 * b + 4 * q
                    first = ((c // CK) * depth + CK * full + (c % CK) // 2) * rows + n
                    out_ref[pl.ds(first, 2, stride=rows), :] = values[4 * q : 4 * q + 2]


def pack_amplitudes_kernel(slots, occ, vir, t_ref, out_ref, chosen_ref):
    step = pl.program_id(0)
    keys = layout(slots)

    @pl.when(step == 0)
    def _():
        first_i = NI * (YL * lax.axis_index("z") + lax.axis_index("yl"))
        first_j = NI * lax.axis_index("ja")

        pair = lax.broadcasted_iota(jnp.int32, (PAIRS, 8, LANES), 0)
        labels = jnp.zeros(pair.shape, jnp.int32)
        for p in range(PAIRS):
            labels = jnp.where(pair == p, occ[first_i + p // NI] ^ occ[first_j + p % NI], labels)

        @pl.loop(0, NVT)
        def _(tc):
            for n, key in enumerate(keys):
                chosen_ref[tc, n, 0], chosen_ref[tc, n, 1] = straight_and_turned(slot_tiles(labels ^ vir[tc], vir, key))

    @pl.loop(0, GROUP)
    def _(g):
        for b in range(CB // 8):
            tc = ((step * GROUP + g) * (CB // 8) + b) // (VT // 8)
            chosen_of = {key: (chosen_ref[tc, n, 0], chosen_ref[tc, n, 1]) for n, key in enumerate(keys)}
            packed = pack_tiles(t_ref[:, pl.ds(pl.multiple_of(g * CB + b * 8, 8), 8), :], chosen_of)
            store_tiles(slots, PAIRS, b, packed, out_ref.at[g])


def pack_amplitudes(amplitudes, occ_irrep, vir_irrep, slots):
    rows = YL * lane_tiles(slots) * PAIRS
    return pl.pallas_call(
        functools.partial(pack_amplitudes_kernel, slots),
        out_shape=jax.ShapeDtypeStruct((JA, rows, LANES), jnp.float32),
        grid=(JA // GROUP,),
        in_specs=[
            pl.BlockSpec(memory_space=pltpu.SMEM),
            pl.BlockSpec(memory_space=pltpu.SMEM),
            pl.BlockSpec((PAIRS, GROUP * CB, NV), lambda s: (0, s, 0)),
        ],
        out_specs=pl.BlockSpec((GROUP, rows, LANES), lambda s: (s, 0, 0)),
        scratch_shapes=[pltpu.VMEM((NVT, len(layout(slots)), 2, PAIRS, 8, LANES), jnp.int32)],
        compiler_params=pltpu.CompilerParams(vmem_limit_bytes=20 * MIB),
        cost_estimate=pl.CostEstimate(flops=10**7, bytes_accessed=14 * 10**6, transcendentals=0),
    )(occ_irrep, vir_irrep, amplitudes.reshape(PAIRS, NV, NV))


def pack_integrals_kernel(slots, vir, v_ref, kept_ref, sent_ref, packed_ref):
    ia = YL * lax.axis_index("z") + lax.axis_index("yl")
    tb = (AB * (ia % (Z * YL // SA)) + 16 * pl.program_id(0)) // VT
    for b in range(CB // 8):
        tc = (lax.axis_index("ja") * (CB // 8) + b) // (VT // 8)
        wanted = jnp.full((8, LANES), vir[0] ^ vir[tb] ^ vir[tc], jnp.int32)
        chosen_of = {key: straight_and_turned(slot_tiles(wanted, vir, key)) for key in layout(slots)}
        store_tiles(slots, 16, b, pack_tiles(v_ref[:, b * 8 : (b + 1) * 8, :], chosen_of), packed_ref)
    depth = lane_tiles(slots) * 16
    for yl, ref in ((lax.axis_index("yl"), kept_ref), (1 - lax.axis_index("yl"), sent_ref)):
        ref[...] = packed_ref[pl.ds(pl.multiple_of(yl * depth, 16), depth), :].reshape(ref.shape)


def pack_integrals(integrals, vir_irrep, slots):
    depth = lane_tiles(slots)
    return pl.pallas_call(
        functools.partial(pack_integrals_kernel, slots),
        out_shape=[jax.ShapeDtypeStruct((depth, AB, LANES), jnp.float32)] * 2,
        grid=(AB // 16,),
        in_specs=[
            pl.BlockSpec(memory_space=pltpu.SMEM),
            pl.BlockSpec((16, CB, NV), lambda s: (s, 0, 0)),
        ],
        out_specs=[pl.BlockSpec((depth, 16, LANES), lambda s: (0, s, 0))] * 2,
        scratch_shapes=[pltpu.VMEM((YL * depth * 16, LANES), jnp.float32)],
        compiler_params=pltpu.CompilerParams(vmem_limit_bytes=12 * MIB),
        cost_estimate=pl.CostEstimate(flops=10**6, bytes_accessed=3 * 10**6, transcendentals=0),
    )(vir_irrep, integrals)


def split(values):
    high = values.astype(jnp.bfloat16)
    return high, (values - high.astype(jnp.float32)).astype(jnp.bfloat16)


def dot(left, right, right_dim):
    return lax.dot_general(left, right, (((1,), (right_dim,)), ((), ())), preferred_element_type=jnp.float32)


def place(values, chosen, right_dim):
    terms = dot(jnp.concatenate(split(values), axis=0), chosen, right_dim)
    return terms[: values.shape[0]] + terms[values.shape[0] :]


def kept_rows(labels, wanted):
    at = lax.broadcasted_iota(jnp.int32, (8, ROWS), 0)
    label_of = jnp.zeros((8, ROWS), jnp.int32)
    for n, label in enumerate(wanted):
        label_of = jnp.where(at == n, label, label_of)
    match = (label_of == labels) & (at < len(wanted))
    before = lax.broadcasted_iota(jnp.int32, (ROWS, ROWS), 0) < lax.broadcasted_iota(jnp.int32, (ROWS, ROWS), 1)
    rank = dot(jnp.where(match, 1.0, 0.0).astype(jnp.bfloat16), jnp.where(before, 1.0, 0.0).astype(jnp.bfloat16), 0)
    rank = jnp.where(match, rank.astype(jnp.int32), -ROWS)
    slot = lax.broadcasted_iota(jnp.int32, (LANES, ROWS), 0)
    return [
        [jnp.where(rank[n : n + 1] + shift == slot, 1.0, 0.0).astype(jnp.bfloat16) for shift in (0, KEPT)]
        for n in range(len(wanted))
    ]


HOPS = [(other, side * n) for n in range(1, 4) for other in range(YL) for side in (1, -1)] + [(0, 4), (1, -4)]
RING = sorted([(0, 0), (1, 0)] + HOPS, key=lambda of: (of[1] % Z, of[0]))
BLOCKS = SA * NV // 16
TILE_BLOCKS = VT // 16


def contract_kernel(keep_all, vir, labels_ref, t_ref, *refs):
    v_refs, (out_ref, v_held, sem, v_high, v_low, t_high, t_low, sums_ref, kept_ref) = refs[:-9], refs[-9:]
    depth = t_ref.shape[2]

    copies, first = [], 0
    for v_ref in v_refs:
        copies.append(pltpu.make_async_copy(v_ref, v_held.at[pl.ds(first, v_ref.shape[0])], sem.at[first]))
        first += v_ref.shape[0]

    @pl.when(pl.program_id(0) == 0)
    def _():
        for copy in copies:
            copy.start()

    labels = labels_ref[0]
    wanted = [vir[0] ^ vir[tb] for tb in range(NVT)]
    if not keep_all:
        for tb, matrices in enumerate(kept_rows(labels, wanted)):
            for n, matrix in enumerate(matrices):
                kept_ref[tb, :, n * ROWS : (n + 1) * ROWS] = matrix

    @pl.loop(0, depth)
    def _(k):
        at = pl.ds(pl.multiple_of(k * LANES, LANES), LANES)
        t_high[:, at], t_low[:, at] = split(t_ref[:, 0, k].reshape(ROWS, LANES))

    @pl.when(pl.program_id(0) == 0)
    def _():
        for copy in copies:
            copy.wait()

        @pl.loop(0, depth)
        def _(k):
            at = pl.ds(pl.multiple_of(k * LANES, LANES), LANES)
            v_high[:, at], v_low[:, at] = split(v_held[:, k].reshape(SA * NV, LANES))

    part = 384

    @pl.loop(0, SA * NV // part)
    def _(m):
        at = pl.ds(pl.multiple_of(m * part, part), part)
        high, low = v_high[at], v_low[at]
        total = dot(high, t_high[...], 1) + dot(high, t_low[...], 1) + dot(low, t_high[...], 1)
        sums_ref[pl.ds(m * (part // 16), part // 16)] = total.reshape(part // 16, 16, ROWS)

    z, yl = lax.axis_index("z"), lax.axis_index("yl")

    def sums_at(block):
        source = block // 3
        return 3 * (YL * lax.rem(z - source // YL + Z, Z) + (yl ^ (source % YL))) + block % 3

    if keep_all:
        for n in range(BLOCKS):
            kept = jnp.where(labels == wanted[n % (BLOCKS // SA) // TILE_BLOCKS], sums_ref[sums_at(n)], 0.0)
            out_ref[0, n // 3, 16 * (n % 3) : 16 * (n % 3) + 16, :] = kept
        return
    for tb in range(NVT):
        blocks = [a * (BLOCKS // SA) + tb * TILE_BLOCKS + q for a in range(SA) for q in range(TILE_BLOCKS)]
        sums = [sums_ref[sums_at(n)] for n in blocks]
        sums = jnp.concatenate([jnp.concatenate([each[:8], each[8:]], axis=1) for each in sums], axis=0)
        kept = place(sums, kept_ref[tb], 1)
        for m, n in enumerate(blocks):
            out_ref[0, n // 3, 8 * (n % 3) : 8 * (n % 3) + 8, :] = kept[8 * m : 8 * m + 8]


def contract(received, ring, labels, vir_irrep, slots, keep_all):
    depth = lane_tiles(slots)
    rest = (AB, ROWS) if keep_all else (AB // 2, LANES)
    return pl.pallas_call(
        functools.partial(contract_kernel, keep_all),
        out_shape=jax.ShapeDtypeStruct((YL, JA) + rest, jnp.float32),
        grid=(YL,),
        in_specs=[
            pl.BlockSpec(memory_space=pltpu.SMEM),
            pl.BlockSpec((1, 1, ROWS), lambda s: (s, 0, 0)),
            pl.BlockSpec((JA, 1, depth, PAIRS, LANES), lambda s: (0, s, 0, 0, 0)),
        ]
        + [pl.BlockSpec(memory_space=pl.ANY)] * len(ring),
        out_specs=pl.BlockSpec((1, JA) + rest, lambda s: (s, 0, 0, 0)),
        scratch_shapes=[pltpu.VMEM((Z * YL, depth, AB, LANES), jnp.float32), pltpu.SemaphoreType.DMA((Z * YL,))]
        + [pltpu.VMEM((Z * YL * AB, depth * LANES), jnp.bfloat16)] * 2
        + [pltpu.VMEM((ROWS, depth * LANES), jnp.bfloat16)] * 2
        + [pltpu.VMEM((BLOCKS, 16, ROWS), jnp.float32), pltpu.VMEM((NVT, LANES, 2 * ROWS), jnp.bfloat16)],
        compiler_params=pltpu.CompilerParams(vmem_limit_bytes=60 * MIB),
        cost_estimate=pl.CostEstimate(flops=6 * 768 * 512 * LANES * depth, bytes_accessed=10**7, transcendentals=0),
    )(vir_irrep, labels, received, *ring)


def reduce_kernel(keep_all, vir, labels_ref, parts_ref, out_ref):
    total = parts_ref[0]
    for n in range(1, YL * JA):
        total += parts_ref[n]
    if keep_all:
        rows = [total]
    else:
        first_block = lax.axis_index("ja") * (AB // 16)
        wanted = [vir[0] ^ vir[(first_block + g) % (BLOCKS // SA) // TILE_BLOCKS] for g in range(AB // 16)]
        rows = []
        for g, chosen in enumerate(kept_rows(labels_ref[lax.axis_index("yl")], wanted)):
            rows += [place(total[8 * g : 8 * g + 8], each, 0) for each in chosen]
    out_ref[...] = jnp.concatenate(rows + [jnp.zeros((LANES - AB, ROWS), jnp.float32)], axis=0).T


def reduce_parts(parts, labels, vir_irrep, keep_all):
    whole = pl.BlockSpec(memory_space=pltpu.VMEM)
    return pl.pallas_call(
        functools.partial(reduce_kernel, keep_all),
        out_shape=jax.ShapeDtypeStruct((ROWS, LANES), jnp.float32),
        in_specs=[pl.BlockSpec(memory_space=pltpu.SMEM), whole, whole],
        out_specs=whole,
        compiler_params=pltpu.CompilerParams(vmem_limit_bytes=12 * MIB),
    )(vir_irrep, labels, parts)


def finish(ladder, occ_energy, vir_energy):
    z, yl, ja = lax.axis_index("z"), lax.axis_index("yl"), lax.axis_index("ja")
    mirror = lax.all_to_all(ladder, ("z", "yl"), split_axis=0, concat_axis=0, tiled=True)
    ladder = ladder.reshape(JA, NI, NI, LANES)[..., :AB].transpose(1, 0, 2, 3).reshape(NI, O, AB)
    mirror = mirror.reshape(JA, NI, NI, LANES)[..., :AB].transpose(2, 0, 1, 3).reshape(NI, O, AB)
    ab_energy = (vir_energy[:SA, None] + vir_energy[None, :]).reshape(SA * NV)
    ab_part = lax.dynamic_slice_in_dim(ab_energy, ja * AB, AB)
    occ_part = lax.dynamic_slice_in_dim(occ_energy, NI * (YL * z + yl), NI)
    denominator = occ_part[:, None, None] + occ_energy[None, :, None] - ab_part[None, None, :]
    return (ladder - mirror) / denominator


def ladder_rows(slots, whole, keep_all, amplitudes, integrals, occ_irrep, vir_irrep):
    forward = [(n, (n + 1) % Z) for n in range(Z)]
    backward = [(n, (n - 1) % Z) for n in range(Z)]
    kept, sent = pack_integrals(integrals, vir_irrep, slots)
    neighbours = lax.ppermute(sent, "yl", [(0, 1), (1, 0)])
    if keep_all:
        both, occ_irrep = lax.optimization_barrier((jnp.stack([kept, neighbours]), occ_irrep))
        packed = pack_amplitudes(amplitudes, occ_irrep, vir_irrep, slots)

        def turn(n, carried):
            behind, ahead, blocks = carried
            behind, ahead = lax.ppermute(behind, "z", forward), lax.ppermute(ahead, "z", backward)
            blocks = lax.dynamic_update_index_in_dim(blocks, behind, n, 0)
            return behind, ahead, lax.dynamic_update_index_in_dim(blocks, ahead, Z - n, 0)

        blocks = jnp.broadcast_to(both, (Z,) + both.shape)
        blocks = lax.fori_loop(1, Z // 2 + 1, turn, (both, both, blocks))[2]
        ring = [blocks.reshape((Z * YL,) + kept.shape)]
    elif whole:
        packed = pack_amplitudes(amplitudes, occ_irrep, vir_irrep, slots)
        packed, neighbours = lax.optimization_barrier((packed, neighbours))
        blocks = {0: jnp.stack([kept, neighbours])}
        for n in range(1, Z // 2):
            blocks[n] = lax.ppermute(blocks[n - 1], "z", forward)
            blocks[-n] = lax.ppermute(blocks[1 - n], "z", backward)
        last = [lax.ppermute(blocks[3][:1], "z", forward), lax.ppermute(blocks[-3][1:], "z", backward)]
        ring = [*(blocks[n] for n in range(Z // 2)), *last, *(blocks[n - Z // 2] for n in range(1, Z // 2))]
    else:
        ring = {(0, 0): kept, (1, 0): neighbours}

        def hop(other, behind):
            side = 1 if behind > 0 else -1
            ring[other, behind] = lax.ppermute(ring[other, behind - side], "z", forward if side > 0 else backward)

        for of in HOPS[:2]:
            hop(*of)
        packed = pack_amplitudes(amplitudes, occ_irrep, vir_irrep, slots)
        packed, ring[1, 0], ring[0, 1], ring[0, -1] = lax.optimization_barrier((packed, ring[1, 0], ring[0, 1], ring[0, -1]))
        for of in HOPS[2:]:
            hop(*of)
        ring = [ring[key][None] for key in RING]
    received = lax.all_to_all(
        packed.reshape(JA * YL, lane_tiles(slots) * PAIRS, LANES), ("ja", "yl"), split_axis=0, concat_axis=0, tiled=True
    ).reshape(JA, YL, lane_tiles(slots), PAIRS, LANES)
    occ_rows = lax.dynamic_slice_in_dim(occ_irrep, YL * NI * lax.axis_index("z"), YL * NI).reshape(YL, 1, NI, 1)
    labels = jnp.bitwise_xor(occ_rows, occ_irrep.reshape(1, JA, 1, NI)).reshape(YL, 1, ROWS)
    parts = contract(received, ring, labels, vir_irrep, slots, keep_all)
    parts = lax.all_to_all(
        parts.reshape((YL * JA,) + parts.shape[2:]), ("yl", "ja"), split_axis=0, concat_axis=0, tiled=True
    )
    return reduce_parts(parts, labels, vir_irrep, keep_all)


def tier_kernel(occ, vir, out_ref):
    def largest_class(ref):
        def count(n, counts):
            one = lax.shift_left(1, 8 * (ref[n] & 3))
            return counts[0] + jnp.where(ref[n] < 4, one, 0), counts[1] + jnp.where(ref[n] < 4, 0, one)

        counts = lax.fori_loop(0, ref.shape[0], count, (jnp.int32(0), jnp.int32(0)), unroll=True)
        largest = jnp.int32(0)
        for four in counts:
            for n in range(4):
                largest = jnp.maximum(largest, lax.shift_right_logical(four, 8 * n) & 255)
        return largest

    out_ref[0] = jnp.where(largest_class(occ) <= KEPT // NI, jnp.minimum(jnp.maximum(largest_class(vir) - 2, 0), 2), 2)


def local(amplitudes, integrals, occ_irrep, vir_irrep, occ_energy, vir_energy):
    scalars = pl.BlockSpec(memory_space=pltpu.SMEM)
    tier = pl.pallas_call(
        tier_kernel, out_shape=jax.ShapeDtypeStruct((1,), jnp.int32), in_specs=[scalars] * 2, out_specs=scalars
    )(occ_irrep, vir_irrep)
    branches = [functools.partial(ladder_rows, *of) for of in ((2, False, False), (3, True, False), (NVT, True, True))]
    ladder = lax.switch(tier[0], branches, amplitudes, integrals, occ_irrep, vir_irrep)
    return finish(ladder.reshape(JA, PAIRS, LANES), occ_energy, vir_energy)


def solution(mesh):
    parts = Mesh(mesh.devices.reshape(Z, YL, JA), ("z", "yl", "ja"))
    rows = ("z", "yl")
    in_specs = (P(rows, "ja", None, None), P(rows, "ja", None), P(), P(), P(), P())
    return jax.shard_map(local, mesh=parts, in_specs=in_specs, out_specs=P(rows, None, "ja"), check_vma=False)
```

```python
import functools

import jax
import jax.numpy as jnp
from jax import lax
from jax.experimental import pallas as pl
from jax.experimental.pallas import tpu as pltpu
from jax.sharding import Mesh, PartitionSpec as P

O = 64
NV = 384
VT = 64
SA = 2
NVT = NV // VT
Z = 8
YL = 2
JA = 16
NI = 4
PAIRS = NI * NI
CB = NV // JA
CK = CB // YL
AB = SA * NV // (Z * YL)
ROWS = JA * PAIRS
GROUP = 4
LANES = 128
MIB = 1024 * 1024
KEPT = 64


def layout(slots):
    return [(2 * t, 2 * t + 1) for t in range(slots // 2)] + [(slots - 1, slots - 1)] * (slots % 2)


def lane_tiles(slots):
    return CK * slots // 2


def slot_tiles(wanted, vir, slots):
    lane = lax.broadcasted_iota(jnp.int32, wanted.shape, wanted.ndim - 1)
    slot = jnp.where(lane < VT, slots[0], slots[1])
    count = jnp.zeros(wanted.shape, jnp.int32)
    chosen = jnp.full(wanted.shape, -1, jnp.int32)
    for td in range(NVT):
        match = wanted == vir[td]
        chosen = jnp.where(match & (count == slot), td, chosen)
        count = jnp.where(match, count + 1, count)
    return chosen


def straight_and_turned(chosen):
    half = (lax.broadcasted_iota(jnp.int32, chosen.shape, chosen.ndim - 1) >= VT).astype(jnp.int32)
    return [
        jnp.where((each >= 0) & ((each & 1) == half), each >> 1, -1)
        for each in (chosen, pltpu.roll(chosen, VT, chosen.ndim - 1))
    ]


def pack_tiles(block, chosen_of):
    packed = {}
    for key, chosen in chosen_of.items():
        terms = []
        for each in chosen:
            term = jnp.zeros(block.shape[:2] + (LANES,), jnp.float32)
            for k in range(NV // LANES):
                term = jnp.where(each == k, block[:, :, k * LANES : (k + 1) * LANES], term)
            terms.append(term)
        packed[key] = terms[0] + pltpu.roll(terms[1], VT, 2)
    return packed


def store_tiles(slots, rows, b, packed, out_ref):
    full = slots // 2
    depth = lane_tiles(slots)

    def store(c, tile, values):
        out_ref[pl.ds(((c // CK) * depth + tile) * rows, rows), :] = values

    for t, key in enumerate(layout(slots)):
        values = packed[key]
        if t == full:
            low = lax.broadcasted_iota(jnp.int32, values.shape, 2) < VT
            values = jnp.where(low, values, pltpu.roll(values, 6, 1))
        values = jnp.swapaxes(values, 0, 1)
        for r in range(8):
            c = 8 * b + r
            if t < full:
                store(c, (c % CK) * full + t, values[r])
            elif r % 4 < 2:
                store(c, CK * full + (c % CK) // 4 * 2 + r % 4, values[r])


def pack_amplitudes_kernel(slots, occ, vir, t_ref, out_ref, chosen_ref):
    step = pl.program_id(0)
    keys = layout(slots)

    @pl.when(step == 0)
    def _():
        first_i = NI * (YL * lax.axis_index("z") + lax.axis_index("yl"))
        first_j = NI * lax.axis_index("ja")

        pair = lax.broadcasted_iota(jnp.int32, (PAIRS, 8, LANES), 0)
        labels = jnp.zeros(pair.shape, jnp.int32)
        for p in range(PAIRS):
            labels = jnp.where(pair == p, occ[first_i + p // NI] ^ occ[first_j + p % NI], labels)

        @pl.loop(0, NVT)
        def _(tc):
            for n, key in enumerate(keys):
                chosen_ref[tc, n, 0], chosen_ref[tc, n, 1] = straight_and_turned(slot_tiles(labels ^ vir[tc], vir, key))

    @pl.loop(0, GROUP)
    def _(g):
        for b in range(CB // 8):
            tc = ((step * GROUP + g) * (CB // 8) + b) // (VT // 8)
            chosen_of = {key: (chosen_ref[tc, n, 0], chosen_ref[tc, n, 1]) for n, key in enumerate(keys)}
            packed = pack_tiles(t_ref[:, pl.ds(pl.multiple_of(g * CB + b * 8, 8), 8), :], chosen_of)
            store_tiles(slots, PAIRS, b, packed, out_ref.at[g])


def pack_amplitudes(amplitudes, occ_irrep, vir_irrep, slots):
    rows = YL * lane_tiles(slots) * PAIRS
    return pl.pallas_call(
        functools.partial(pack_amplitudes_kernel, slots),
        out_shape=jax.ShapeDtypeStruct((JA, rows, LANES), jnp.float32),
        grid=(JA // GROUP,),
        in_specs=[
            pl.BlockSpec(memory_space=pltpu.SMEM),
            pl.BlockSpec(memory_space=pltpu.SMEM),
            pl.BlockSpec((PAIRS, GROUP * CB, NV), lambda s: (0, s, 0)),
        ],
        out_specs=pl.BlockSpec((GROUP, rows, LANES), lambda s: (s, 0, 0)),
        scratch_shapes=[pltpu.VMEM((NVT, len(layout(slots)), 2, PAIRS, 8, LANES), jnp.int32)],
        compiler_params=pltpu.CompilerParams(vmem_limit_bytes=20 * MIB),
        cost_estimate=pl.CostEstimate(flops=10**7, bytes_accessed=14 * 10**6, transcendentals=0),
    )(occ_irrep, vir_irrep, amplitudes.reshape(PAIRS, NV, NV))


def pack_integrals_kernel(slots, vir, v_ref, kept_ref, sent_ref, packed_ref):
    ia = YL * lax.axis_index("z") + lax.axis_index("yl")
    tb = (AB * (ia % (Z * YL // SA)) + 16 * pl.program_id(0)) // VT
    for b in range(CB // 8):
        tc = (lax.axis_index("ja") * (CB // 8) + b) // (VT // 8)
        wanted = jnp.full((8, LANES), vir[0] ^ vir[tb] ^ vir[tc], jnp.int32)
        chosen_of = {key: straight_and_turned(slot_tiles(wanted, vir, key)) for key in layout(slots)}
        store_tiles(slots, 16, b, pack_tiles(v_ref[:, b * 8 : (b + 1) * 8, :], chosen_of), packed_ref)
    depth = lane_tiles(slots) * 16
    for yl, ref in ((lax.axis_index("yl"), kept_ref), (1 - lax.axis_index("yl"), sent_ref)):
        ref[...] = packed_ref[pl.ds(pl.multiple_of(yl * depth, 16), depth), :].reshape(ref.shape)


def pack_integrals(integrals, vir_irrep, slots):
    depth = lane_tiles(slots)
    return pl.pallas_call(
        functools.partial(pack_integrals_kernel, slots),
        out_shape=[jax.ShapeDtypeStruct((depth, AB, LANES), jnp.float32)] * 2,
        grid=(AB // 16,),
        in_specs=[
            pl.BlockSpec(memory_space=pltpu.SMEM),
            pl.BlockSpec((16, CB, NV), lambda s: (s, 0, 0)),
        ],
        out_specs=[pl.BlockSpec((depth, 16, LANES), lambda s: (0, s, 0))] * 2,
        scratch_shapes=[pltpu.VMEM((YL * depth * 16, LANES), jnp.float32)],
        compiler_params=pltpu.CompilerParams(vmem_limit_bytes=12 * MIB),
        cost_estimate=pl.CostEstimate(flops=10**6, bytes_accessed=3 * 10**6, transcendentals=0),
    )(vir_irrep, integrals)


def split(values):
    high = values.astype(jnp.bfloat16)
    return high, (values - high.astype(jnp.float32)).astype(jnp.bfloat16)


def dot(left, right, right_dim):
    return lax.dot_general(left, right, (((1,), (right_dim,)), ((), ())), preferred_element_type=jnp.float32)


def place(values, chosen, right_dim):
    terms = dot(jnp.concatenate(split(values), axis=0), chosen, right_dim)
    return terms[: values.shape[0]] + terms[values.shape[0] :]


def kept_rows(labels, wanted):
    at = lax.broadcasted_iota(jnp.int32, (8, ROWS), 0)
    label_of = jnp.zeros((8, ROWS), jnp.int32)
    for n, label in enumerate(wanted):
        label_of = jnp.where(at == n, label, label_of)
    match = (label_of == labels) & (at < len(wanted))
    before = lax.broadcasted_iota(jnp.int32, (ROWS, ROWS), 0) < lax.broadcasted_iota(jnp.int32, (ROWS, ROWS), 1)
    rank = dot(jnp.where(match, 1.0, 0.0).astype(jnp.bfloat16), jnp.where(before, 1.0, 0.0).astype(jnp.bfloat16), 0)
    rank = jnp.where(match, rank.astype(jnp.int32), -ROWS)
    slot = lax.broadcasted_iota(jnp.int32, (LANES, ROWS), 0)
    return [
        [jnp.where(rank[n : n + 1] + shift == slot, 1.0, 0.0).astype(jnp.bfloat16) for shift in (0, KEPT)]
        for n in range(len(wanted))
    ]


HOPS = [(other, side * n) for n in range(1, 4) for other in range(YL) for side in (1, -1)] + [(0, 4), (1, -4)]
RING = sorted([(0, 0), (1, 0)] + HOPS, key=lambda of: (of[1] % Z, of[0]))
BLOCKS = SA * NV // 16
TILE_BLOCKS = VT // 16


def contract_kernel(keep_all, vir, labels_ref, t_ref, *refs):
    v_refs, (out_ref, v_held, sem, v_high, v_low, t_high, t_low, sums_ref, kept_ref) = refs[:-9], refs[-9:]
    depth = t_ref.shape[2]

    copies, first = [], 0
    for v_ref in v_refs:
        copies.append(pltpu.make_async_copy(v_ref, v_held.at[pl.ds(first, v_ref.shape[0])], sem.at[first]))
        first += v_ref.shape[0]

    @pl.when(pl.program_id(0) == 0)
    def _():
        for copy in copies:
            copy.start()

    labels = labels_ref[0]
    wanted = [vir[0] ^ vir[tb] for tb in range(NVT)]
    if not keep_all:
        for tb, matrices in enumerate(kept_rows(labels, wanted)):
            for n, matrix in enumerate(matrices):
                kept_ref[tb, :, n * ROWS : (n + 1) * ROWS] = matrix

    @pl.loop(0, depth)
    def _(k):
        at = pl.ds(pl.multiple_of(k * LANES, LANES), LANES)
        t_high[:, at], t_low[:, at] = split(t_ref[:, 0, k].reshape(ROWS, LANES))

    @pl.when(pl.program_id(0) == 0)
    def _():
        for copy in copies:
            copy.wait()

        @pl.loop(0, depth)
        def _(k):
            at = pl.ds(pl.multiple_of(k * LANES, LANES), LANES)
            v_high[:, at], v_low[:, at] = split(v_held[:, k].reshape(SA * NV, LANES))

    part = 384

    @pl.loop(0, SA * NV // part)
    def _(m):
        at = pl.ds(pl.multiple_of(m * part, part), part)
        high, low = v_high[at], v_low[at]
        total = dot(high, t_high[...], 1) + dot(high, t_low[...], 1) + dot(low, t_high[...], 1)
        sums_ref[pl.ds(m * (part // 16), part // 16)] = total.reshape(part // 16, 16, ROWS)

    z, yl = lax.axis_index("z"), lax.axis_index("yl")

    def sums_at(block):
        source = block // 3
        return 3 * (YL * lax.rem(z - source // YL + Z, Z) + (yl ^ (source % YL))) + block % 3

    if keep_all:
        for n in range(BLOCKS):
            kept = jnp.where(labels == wanted[n % (BLOCKS // SA) // TILE_BLOCKS], sums_ref[sums_at(n)], 0.0)
            out_ref[0, n // 3, 16 * (n % 3) : 16 * (n % 3) + 16, :] = kept
        return
    for tb in range(NVT):
        blocks = [a * (BLOCKS // SA) + tb * TILE_BLOCKS + q for a in range(SA) for q in range(TILE_BLOCKS)]
        sums = [sums_ref[sums_at(n)] for n in blocks]
        sums = jnp.concatenate([jnp.concatenate([each[:8], each[8:]], axis=1) for each in sums], axis=0)
        kept = place(sums, kept_ref[tb], 1)
        for m, n in enumerate(blocks):
            out_ref[0, n // 3, 8 * (n % 3) : 8 * (n % 3) + 8, :] = kept[8 * m : 8 * m + 8]


def contract(received, ring, labels, vir_irrep, slots, keep_all):
    depth = lane_tiles(slots)
    rest = (AB, ROWS) if keep_all else (AB // 2, LANES)
    return pl.pallas_call(
        functools.partial(contract_kernel, keep_all),
        out_shape=jax.ShapeDtypeStruct((YL, JA) + rest, jnp.float32),
        grid=(YL,),
        in_specs=[
            pl.BlockSpec(memory_space=pltpu.SMEM),
            pl.BlockSpec((1, 1, ROWS), lambda s: (s, 0, 0)),
            pl.BlockSpec((JA, 1, depth, PAIRS, LANES), lambda s: (0, s, 0, 0, 0)),
        ]
        + [pl.BlockSpec(memory_space=pl.ANY)] * len(ring),
        out_specs=pl.BlockSpec((1, JA) + rest, lambda s: (s, 0, 0, 0)),
        scratch_shapes=[pltpu.VMEM((Z * YL, depth, AB, LANES), jnp.float32), pltpu.SemaphoreType.DMA((Z * YL,))]
        + [pltpu.VMEM((Z * YL * AB, depth * LANES), jnp.bfloat16)] * 2
        + [pltpu.VMEM((ROWS, depth * LANES), jnp.bfloat16)] * 2
        + [pltpu.VMEM((BLOCKS, 16, ROWS), jnp.float32), pltpu.VMEM((NVT, LANES, 2 * ROWS), jnp.bfloat16)],
        compiler_params=pltpu.CompilerParams(vmem_limit_bytes=60 * MIB),
        cost_estimate=pl.CostEstimate(flops=6 * 768 * 512 * LANES * depth, bytes_accessed=10**7, transcendentals=0),
    )(vir_irrep, labels, received, *ring)


def reduce_kernel(keep_all, vir, labels_ref, parts_ref, out_ref):
    total = parts_ref[0]
    for n in range(1, YL * JA):
        total += parts_ref[n]
    if keep_all:
        rows = [total]
    else:
        first_block = lax.axis_index("ja") * (AB // 16)
        wanted = [vir[0] ^ vir[(first_block + g) % (BLOCKS // SA) // TILE_BLOCKS] for g in range(AB // 16)]
        rows = []
        for g, chosen in enumerate(kept_rows(labels_ref[lax.axis_index("yl")], wanted)):
            rows += [place(total[8 * g : 8 * g + 8], each, 0) for each in chosen]
    out_ref[...] = jnp.concatenate(rows + [jnp.zeros((LANES - AB, ROWS), jnp.float32)], axis=0).T


def reduce_parts(parts, labels, vir_irrep, keep_all):
    whole = pl.BlockSpec(memory_space=pltpu.VMEM)
    return pl.pallas_call(
        functools.partial(reduce_kernel, keep_all),
        out_shape=jax.ShapeDtypeStruct((ROWS, LANES), jnp.float32),
        in_specs=[pl.BlockSpec(memory_space=pltpu.SMEM), whole, whole],
        out_specs=whole,
        compiler_params=pltpu.CompilerParams(vmem_limit_bytes=12 * MIB),
    )(vir_irrep, labels, parts)


def finish(ladder, occ_energy, vir_energy):
    z, yl, ja = lax.axis_index("z"), lax.axis_index("yl"), lax.axis_index("ja")
    mirror = lax.all_to_all(ladder, ("z", "yl"), split_axis=0, concat_axis=0, tiled=True)
    ladder = ladder.reshape(JA, NI, NI, LANES)[..., :AB].transpose(1, 0, 2, 3).reshape(NI, O, AB)
    mirror = mirror.reshape(JA, NI, NI, LANES)[..., :AB].transpose(2, 0, 1, 3).reshape(NI, O, AB)
    ab_energy = (vir_energy[:SA, None] + vir_energy[None, :]).reshape(SA * NV)
    ab_part = lax.dynamic_slice_in_dim(ab_energy, ja * AB, AB)
    occ_part = lax.dynamic_slice_in_dim(occ_energy, NI * (YL * z + yl), NI)
    denominator = occ_part[:, None, None] + occ_energy[None, :, None] - ab_part[None, None, :]
    return (ladder - mirror) / denominator


def ladder_rows(slots, whole, keep_all, amplitudes, integrals, occ_irrep, vir_irrep):
    forward = [(n, (n + 1) % Z) for n in range(Z)]
    backward = [(n, (n - 1) % Z) for n in range(Z)]
    kept, sent = pack_integrals(integrals, vir_irrep, slots)
    neighbours = lax.ppermute(sent, "yl", [(0, 1), (1, 0)])
    if keep_all:
        both, occ_irrep = lax.optimization_barrier((jnp.stack([kept, neighbours]), occ_irrep))
        packed = pack_amplitudes(amplitudes, occ_irrep, vir_irrep, slots)

        def turn(n, carried):
            behind, ahead, blocks = carried
            behind, ahead = lax.ppermute(behind, "z", forward), lax.ppermute(ahead, "z", backward)
            blocks = lax.dynamic_update_index_in_dim(blocks, behind, n, 0)
            return behind, ahead, lax.dynamic_update_index_in_dim(blocks, ahead, Z - n, 0)

        blocks = jnp.broadcast_to(both, (Z,) + both.shape)
        blocks = lax.fori_loop(1, Z // 2 + 1, turn, (both, both, blocks))[2]
        ring = [blocks.reshape((Z * YL,) + kept.shape)]
    elif whole:
        packed = pack_amplitudes(amplitudes, occ_irrep, vir_irrep, slots)
        packed, neighbours = lax.optimization_barrier((packed, neighbours))
        blocks = {0: jnp.stack([kept, neighbours])}
        for n in range(1, Z // 2):
            blocks[n] = lax.ppermute(blocks[n - 1], "z", forward)
            blocks[-n] = lax.ppermute(blocks[1 - n], "z", backward)
        last = [lax.ppermute(blocks[3][:1], "z", forward), lax.ppermute(blocks[-3][1:], "z", backward)]
        ring = [*(blocks[n] for n in range(Z // 2)), *last, *(blocks[n - Z // 2] for n in range(1, Z // 2))]
    else:
        ring = {(0, 0): kept, (1, 0): neighbours}

        def hop(other, behind):
            side = 1 if behind > 0 else -1
            ring[other, behind] = lax.ppermute(ring[other, behind - side], "z", forward if side > 0 else backward)

        for of in HOPS[:2]:
            hop(*of)
        packed = pack_amplitudes(amplitudes, occ_irrep, vir_irrep, slots)
        packed, ring[1, 0], ring[0, 1], ring[0, -1] = lax.optimization_barrier((packed, ring[1, 0], ring[0, 1], ring[0, -1]))
        for of in HOPS[2:]:
            hop(*of)
        ring = [ring[key][None] for key in RING]
    received = lax.all_to_all(
        packed.reshape(JA * YL, lane_tiles(slots) * PAIRS, LANES), ("ja", "yl"), split_axis=0, concat_axis=0, tiled=True
    ).reshape(JA, YL, lane_tiles(slots), PAIRS, LANES)
    occ_rows = lax.dynamic_slice_in_dim(occ_irrep, YL * NI * lax.axis_index("z"), YL * NI).reshape(YL, 1, NI, 1)
    labels = jnp.bitwise_xor(occ_rows, occ_irrep.reshape(1, JA, 1, NI)).reshape(YL, 1, ROWS)
    parts = contract(received, ring, labels, vir_irrep, slots, keep_all)
    parts = lax.all_to_all(
        parts.reshape((YL * JA,) + parts.shape[2:]), ("yl", "ja"), split_axis=0, concat_axis=0, tiled=True
    )
    return reduce_parts(parts, labels, vir_irrep, keep_all)


def tier_kernel(occ, vir, out_ref):
    def largest_class(ref):
        def count(n, counts):
            one = lax.shift_left(1, 8 * (ref[n] & 3))
            return counts[0] + jnp.where(ref[n] < 4, one, 0), counts[1] + jnp.where(ref[n] < 4, 0, one)

        counts = lax.fori_loop(0, ref.shape[0], count, (jnp.int32(0), jnp.int32(0)), unroll=True)
        largest = jnp.int32(0)
        for four in counts:
            for n in range(4):
                largest = jnp.maximum(largest, lax.shift_right_logical(four, 8 * n) & 255)
        return largest

    out_ref[0] = jnp.where(largest_class(occ) <= KEPT // NI, jnp.minimum(jnp.maximum(largest_class(vir) - 2, 0), 2), 2)


def local(amplitudes, integrals, occ_irrep, vir_irrep, occ_energy, vir_energy):
    scalars = pl.BlockSpec(memory_space=pltpu.SMEM)
    tier = pl.pallas_call(
        tier_kernel, out_shape=jax.ShapeDtypeStruct((1,), jnp.int32), in_specs=[scalars] * 2, out_specs=scalars
    )(occ_irrep, vir_irrep)
    branches = [functools.partial(ladder_rows, *of) for of in ((2, False, False), (3, True, False), (NVT, True, True))]
    ladder = lax.switch(tier[0], branches, amplitudes, integrals, occ_irrep, vir_irrep)
    return finish(ladder.reshape(JA, PAIRS, LANES), occ_energy, vir_energy)


def solution(mesh):
    parts = Mesh(mesh.devices.reshape(Z, YL, JA), ("z", "yl", "ja"))
    rows = ("z", "yl")
    in_specs = (P(rows, "ja", None, None), P(rows, "ja", None), P(), P(), P(), P())
    return jax.shard_map(local, mesh=parts, in_specs=in_specs, out_specs=P(rows, None, "ja"), check_vma=False)
```

```python
import functools

import jax
import jax.numpy as jnp
from jax import lax
from jax.experimental import pallas as pl
from jax.experimental.pallas import tpu as pltpu
from jax.sharding import Mesh, PartitionSpec as P

O = 64
NV = 384
VT = 64
SA = 2
NVT = NV // VT
Z = 8
YL = 2
JA = 16
NI = 4
PAIRS = NI * NI
CB = NV // JA
CK = CB // YL
AB = SA * NV // (Z * YL)
ROWS = JA * PAIRS
GROUP = 4
LANES = 128
MIB = 1024 * 1024
KEPT = 64


def layout(slots):
    return [(2 * t, 2 * t + 1) for t in range(slots // 2)] + [(slots - 1, slots - 1)] * (slots % 2)


def lane_tiles(slots):
    return CK * slots // 2


def slot_tiles(wanted, vir, slots):
    lane = lax.broadcasted_iota(jnp.int32, wanted.shape, wanted.ndim - 1)
    slot = jnp.where(lane < VT, slots[0], slots[1])
    count = jnp.zeros(wanted.shape, jnp.int32)
    chosen = jnp.full(wanted.shape, -1, jnp.int32)
    for td in range(NVT):
        match = wanted == vir[td]
        chosen = jnp.where(match & (count == slot), td, chosen)
        count = jnp.where(match, count + 1, count)
    return chosen


def straight_and_turned(chosen):
    half = (lax.broadcasted_iota(jnp.int32, chosen.shape, chosen.ndim - 1) >= VT).astype(jnp.int32)
    return [
        jnp.where((each >= 0) & ((each & 1) == half), each >> 1, -1)
        for each in (chosen, pltpu.roll(chosen, VT, chosen.ndim - 1))
    ]


def pack_tiles(block, chosen_of):
    packed = {}
    for key, chosen in chosen_of.items():
        terms = []
        for each in chosen:
            term = jnp.zeros(block.shape[:2] + (LANES,), jnp.float32)
            for k in range(NV // LANES):
                term = jnp.where(each == k, block[:, :, k * LANES : (k + 1) * LANES], term)
            terms.append(term)
        packed[key] = terms[0] + pltpu.roll(terms[1], VT, 2)
    return packed


def store_tiles(slots, rows, b, packed, out_ref):
    full = slots // 2
    depth = lane_tiles(slots)

    def store(c, tile, values):
        out_ref[pl.ds(((c // CK) * depth + tile) * rows, rows), :] = values

    for t, key in enumerate(layout(slots)):
        values = packed[key]
        if t == full:
            low = lax.broadcasted_iota(jnp.int32, values.shape, 2) < VT
            values = jnp.where(low, values, pltpu.roll(values, 6, 1))
        values = jnp.swapaxes(values, 0, 1)
        for r in range(8):
            c = 8 * b + r
            if t < full:
                store(c, (c % CK) * full + t, values[r])
            elif r % 4 < 2:
                store(c, CK * full + (c % CK) // 4 * 2 + r % 4, values[r])


def pack_amplitudes_kernel(slots, occ, vir, t_ref, out_ref, chosen_ref):
    step = pl.program_id(0)
    keys = layout(slots)

    @pl.when(step == 0)
    def _():
        first_i = NI * (YL * lax.axis_index("z") + lax.axis_index("yl"))
        first_j = NI * lax.axis_index("ja")

        pair = lax.broadcasted_iota(jnp.int32, (PAIRS, 8, LANES), 0)
        labels = jnp.zeros(pair.shape, jnp.int32)
        for p in range(PAIRS):
            labels = jnp.where(pair == p, occ[first_i + p // NI] ^ occ[first_j + p % NI], labels)

        @pl.loop(0, NVT)
        def _(tc):
            for n, key in enumerate(keys):
                chosen_ref[tc, n, 0], chosen_ref[tc, n, 1] = straight_and_turned(slot_tiles(labels ^ vir[tc], vir, key))

    @pl.loop(0, GROUP)
    def _(g):
        for b in range(CB // 8):
            tc = ((step * GROUP + g) * (CB // 8) + b) // (VT // 8)
            chosen_of = {key: (chosen_ref[tc, n, 0], chosen_ref[tc, n, 1]) for n, key in enumerate(keys)}
            packed = pack_tiles(t_ref[:, pl.ds(pl.multiple_of(g * CB + b * 8, 8), 8), :], chosen_of)
            store_tiles(slots, PAIRS, b, packed, out_ref.at[g])


def pack_amplitudes(amplitudes, occ_irrep, vir_irrep, slots):
    rows = YL * lane_tiles(slots) * PAIRS
    return pl.pallas_call(
        functools.partial(pack_amplitudes_kernel, slots),
        out_shape=jax.ShapeDtypeStruct((JA, rows, LANES), jnp.float32),
        grid=(JA // GROUP,),
        in_specs=[
            pl.BlockSpec(memory_space=pltpu.SMEM),
            pl.BlockSpec(memory_space=pltpu.SMEM),
            pl.BlockSpec((PAIRS, GROUP * CB, NV), lambda s: (0, s, 0)),
        ],
        out_specs=pl.BlockSpec((GROUP, rows, LANES), lambda s: (s, 0, 0)),
        scratch_shapes=[pltpu.VMEM((NVT, len(layout(slots)), 2, PAIRS, 8, LANES), jnp.int32)],
        compiler_params=pltpu.CompilerParams(vmem_limit_bytes=20 * MIB),
        cost_estimate=pl.CostEstimate(flops=10**7, bytes_accessed=14 * 10**6, transcendentals=0),
    )(occ_irrep, vir_irrep, amplitudes.reshape(PAIRS, NV, NV))


def pack_integrals_kernel(slots, vir, v_ref, kept_ref, sent_ref, packed_ref):
    ia = YL * lax.axis_index("z") + lax.axis_index("yl")
    tb = (AB * (ia % (Z * YL // SA)) + 16 * pl.program_id(0)) // VT
    for b in range(CB // 8):
        tc = (lax.axis_index("ja") * (CB // 8) + b) // (VT // 8)
        wanted = jnp.full((8, LANES), vir[0] ^ vir[tb] ^ vir[tc], jnp.int32)
        chosen_of = {key: straight_and_turned(slot_tiles(wanted, vir, key)) for key in layout(slots)}
        store_tiles(slots, 16, b, pack_tiles(v_ref[:, b * 8 : (b + 1) * 8, :], chosen_of), packed_ref)
    depth = lane_tiles(slots) * 16
    for yl, ref in ((lax.axis_index("yl"), kept_ref), (1 - lax.axis_index("yl"), sent_ref)):
        ref[...] = packed_ref[pl.ds(pl.multiple_of(yl * depth, 16), depth), :].reshape(ref.shape)


def pack_integrals(integrals, vir_irrep, slots):
    depth = lane_tiles(slots)
    return pl.pallas_call(
        functools.partial(pack_integrals_kernel, slots),
        out_shape=[jax.ShapeDtypeStruct((depth, AB, LANES), jnp.float32)] * 2,
        grid=(AB // 16,),
        in_specs=[
            pl.BlockSpec(memory_space=pltpu.SMEM),
            pl.BlockSpec((16, CB, NV), lambda s: (s, 0, 0)),
        ],
        out_specs=[pl.BlockSpec((depth, 16, LANES), lambda s: (0, s, 0))] * 2,
        scratch_shapes=[pltpu.VMEM((YL * depth * 16, LANES), jnp.float32)],
        compiler_params=pltpu.CompilerParams(vmem_limit_bytes=12 * MIB),
        cost_estimate=pl.CostEstimate(flops=10**6, bytes_accessed=3 * 10**6, transcendentals=0),
    )(vir_irrep, integrals)


def split(values):
    high = values.astype(jnp.bfloat16)
    return high, (values - high.astype(jnp.float32)).astype(jnp.bfloat16)


def dot(left, right, right_dim):
    return lax.dot_general(left, right, (((1,), (right_dim,)), ((), ())), preferred_element_type=jnp.float32)


def place(values, chosen, right_dim):
    terms = dot(jnp.concatenate(split(values), axis=0), chosen, right_dim)
    return terms[: values.shape[0]] + terms[values.shape[0] :]


def kept_rows(labels, wanted):
    at = lax.broadcasted_iota(jnp.int32, (8, ROWS), 0)
    label_of = jnp.zeros((8, ROWS), jnp.int32)
    for n, label in enumerate(wanted):
        label_of = jnp.where(at == n, label, label_of)
    match = (label_of == labels) & (at < len(wanted))
    before = lax.broadcasted_iota(jnp.int32, (ROWS, ROWS), 0) < lax.broadcasted_iota(jnp.int32, (ROWS, ROWS), 1)
    rank = dot(jnp.where(match, 1.0, 0.0).astype(jnp.bfloat16), jnp.where(before, 1.0, 0.0).astype(jnp.bfloat16), 0)
    rank = jnp.where(match, rank.astype(jnp.int32), -ROWS)
    slot = lax.broadcasted_iota(jnp.int32, (LANES, ROWS), 0)
    return [
        [jnp.where(rank[n : n + 1] + shift == slot, 1.0, 0.0).astype(jnp.bfloat16) for shift in (0, KEPT)]
        for n in range(len(wanted))
    ]


HOPS = [(other, side * n) for n in range(1, 4) for other in range(YL) for side in (1, -1)] + [(0, 4), (1, -4)]
RING = sorted([(0, 0), (1, 0)] + HOPS, key=lambda of: (of[1] % Z, of[0]))
BLOCKS = SA * NV // 16
TILE_BLOCKS = VT // 16


def contract_kernel(keep_all, vir, labels_ref, t_ref, *refs):
    v_refs, (out_ref, v_held, sem, v_high, v_low, t_high, t_low, sums_ref, kept_ref) = refs[:-9], refs[-9:]
    depth = t_ref.shape[2]

    copies, first = [], 0
    for v_ref in v_refs:
        copies.append(pltpu.make_async_copy(v_ref, v_held.at[pl.ds(first, v_ref.shape[0])], sem.at[first]))
        first += v_ref.shape[0]

    @pl.when(pl.program_id(0) == 0)
    def _():
        for copy in copies:
            copy.start()

    labels = labels_ref[0]
    wanted = [vir[0] ^ vir[tb] for tb in range(NVT)]
    if not keep_all:
        for tb, matrices in enumerate(kept_rows(labels, wanted)):
            for n, matrix in enumerate(matrices):
                kept_ref[tb, :, n * ROWS : (n + 1) * ROWS] = matrix

    @pl.loop(0, depth)
    def _(k):
        at = pl.ds(pl.multiple_of(k * LANES, LANES), LANES)
        t_high[:, at], t_low[:, at] = split(t_ref[:, 0, k].reshape(ROWS, LANES))

    @pl.when(pl.program_id(0) == 0)
    def _():
        for copy in copies:
            copy.wait()

        @pl.loop(0, depth)
        def _(k):
            at = pl.ds(pl.multiple_of(k * LANES, LANES), LANES)
            v_high[:, at], v_low[:, at] = split(v_held[:, k].reshape(SA * NV, LANES))

    part = 384

    @pl.loop(0, SA * NV // part)
    def _(m):
        at = pl.ds(pl.multiple_of(m * part, part), part)
        high, low = v_high[at], v_low[at]
        total = dot(high, t_high[...], 1) + dot(high, t_low[...], 1) + dot(low, t_high[...], 1)
        sums_ref[pl.ds(m * (part // 16), part // 16)] = total.reshape(part // 16, 16, ROWS)

    z, yl = lax.axis_index("z"), lax.axis_index("yl")

    def sums_at(block):
        source = block // 3
        return 3 * (YL * lax.rem(z - source // YL + Z, Z) + (yl ^ (source % YL))) + block % 3

    if keep_all:
        for n in range(BLOCKS):
            kept = jnp.where(labels == wanted[n % (BLOCKS // SA) // TILE_BLOCKS], sums_ref[sums_at(n)], 0.0)
            out_ref[0, n // 3, 16 * (n % 3) : 16 * (n % 3) + 16, :] = kept
        return
    for tb in range(NVT):
        blocks = [a * (BLOCKS // SA) + tb * TILE_BLOCKS + q for a in range(SA) for q in range(TILE_BLOCKS)]
        sums = [sums_ref[sums_at(n)] for n in blocks]
        sums = jnp.concatenate([jnp.concatenate([each[:8], each[8:]], axis=1) for each in sums], axis=0)
        kept = place(sums, kept_ref[tb], 1)
        for m, n in enumerate(blocks):
            out_ref[0, n // 3, 8 * (n % 3) : 8 * (n % 3) + 8, :] = kept[8 * m : 8 * m + 8]


def contract(received, ring, labels, vir_irrep, slots, keep_all):
    depth = lane_tiles(slots)
    rest = (AB, ROWS) if keep_all else (AB // 2, LANES)
    return pl.pallas_call(
        functools.partial(contract_kernel, keep_all),
        out_shape=jax.ShapeDtypeStruct((YL, JA) + rest, jnp.float32),
        grid=(YL,),
        in_specs=[
            pl.BlockSpec(memory_space=pltpu.SMEM),
            pl.BlockSpec((1, 1, ROWS), lambda s: (s, 0, 0)),
            pl.BlockSpec((JA, 1, depth, PAIRS, LANES), lambda s: (0, s, 0, 0, 0)),
        ]
        + [pl.BlockSpec(memory_space=pl.ANY)] * len(ring),
        out_specs=pl.BlockSpec((1, JA) + rest, lambda s: (s, 0, 0, 0)),
        scratch_shapes=[pltpu.VMEM((Z * YL, depth, AB, LANES), jnp.float32), pltpu.SemaphoreType.DMA((Z * YL,))]
        + [pltpu.VMEM((Z * YL * AB, depth * LANES), jnp.bfloat16)] * 2
        + [pltpu.VMEM((ROWS, depth * LANES), jnp.bfloat16)] * 2
        + [pltpu.VMEM((BLOCKS, 16, ROWS), jnp.float32), pltpu.VMEM((NVT, LANES, 2 * ROWS), jnp.bfloat16)],
        compiler_params=pltpu.CompilerParams(vmem_limit_bytes=60 * MIB),
        cost_estimate=pl.CostEstimate(flops=6 * 768 * 512 * LANES * depth, bytes_accessed=10**7, transcendentals=0),
    )(vir_irrep, labels, received, *ring)


def reduce_kernel(keep_all, vir, labels_ref, parts_ref, out_ref):
    total = parts_ref[0]
    for n in range(1, YL * JA):
        total += parts_ref[n]
    if keep_all:
        rows = [total]
    else:
        first_block = lax.axis_index("ja") * (AB // 16)
        wanted = [vir[0] ^ vir[(first_block + g) % (BLOCKS // SA) // TILE_BLOCKS] for g in range(AB // 16)]
        rows = []
        for g, chosen in enumerate(kept_rows(labels_ref[lax.axis_index("yl")], wanted)):
            rows += [place(total[8 * g : 8 * g + 8], each, 0) for each in chosen]
    out_ref[...] = jnp.concatenate(rows + [jnp.zeros((LANES - AB, ROWS), jnp.float32)], axis=0).T


def reduce_parts(parts, labels, vir_irrep, keep_all):
    whole = pl.BlockSpec(memory_space=pltpu.VMEM)
    return pl.pallas_call(
        functools.partial(reduce_kernel, keep_all),
        out_shape=jax.ShapeDtypeStruct((ROWS, LANES), jnp.float32),
        in_specs=[pl.BlockSpec(memory_space=pltpu.SMEM), whole, whole],
        out_specs=whole,
        compiler_params=pltpu.CompilerParams(vmem_limit_bytes=12 * MIB),
    )(vir_irrep, labels, parts)


def finish(ladder, occ_energy, vir_energy):
    z, yl, ja = lax.axis_index("z"), lax.axis_index("yl"), lax.axis_index("ja")
    mirror = lax.all_to_all(ladder, ("z", "yl"), split_axis=0, concat_axis=0, tiled=True)
    ladder = ladder.reshape(JA, NI, NI, LANES)[..., :AB].transpose(1, 0, 2, 3).reshape(NI, O, AB)
    mirror = mirror.reshape(JA, NI, NI, LANES)[..., :AB].transpose(2, 0, 1, 3).reshape(NI, O, AB)
    ab_energy = (vir_energy[:SA, None] + vir_energy[None, :]).reshape(SA * NV)
    ab_part = lax.dynamic_slice_in_dim(ab_energy, ja * AB, AB)
    occ_part = lax.dynamic_slice_in_dim(occ_energy, NI * (YL * z + yl), NI)
    denominator = occ_part[:, None, None] + occ_energy[None, :, None] - ab_part[None, None, :]
    return (ladder - mirror) / denominator


def ladder_rows(slots, whole, keep_all, amplitudes, integrals, occ_irrep, vir_irrep):
    forward = [(n, (n + 1) % Z) for n in range(Z)]
    backward = [(n, (n - 1) % Z) for n in range(Z)]
    kept, sent = pack_integrals(integrals, vir_irrep, slots)
    neighbours = lax.ppermute(sent, "yl", [(0, 1), (1, 0)])
    if keep_all:
        both, occ_irrep = lax.optimization_barrier((jnp.stack([kept, neighbours]), occ_irrep))
        packed = pack_amplitudes(amplitudes, occ_irrep, vir_irrep, slots)

        def turn(n, carried):
            behind, ahead, blocks = carried
            behind, ahead = lax.ppermute(behind, "z", forward), lax.ppermute(ahead, "z", backward)
            blocks = lax.dynamic_update_index_in_dim(blocks, behind, n, 0)
            return behind, ahead, lax.dynamic_update_index_in_dim(blocks, ahead, Z - n, 0)

        blocks = jnp.broadcast_to(both, (Z,) + both.shape)
        blocks = lax.fori_loop(1, Z // 2 + 1, turn, (both, both, blocks))[2]
        ring = [blocks.reshape((Z * YL,) + kept.shape)]
    elif whole:
        packed = pack_amplitudes(amplitudes, occ_irrep, vir_irrep, slots)
        packed, neighbours = lax.optimization_barrier((packed, neighbours))
        blocks = {0: jnp.stack([kept, neighbours])}
        for n in range(1, Z // 2):
            blocks[n] = lax.ppermute(blocks[n - 1], "z", forward)
            blocks[-n] = lax.ppermute(blocks[1 - n], "z", backward)
        last = [lax.ppermute(blocks[3][:1], "z", forward), lax.ppermute(blocks[-3][1:], "z", backward)]
        ring = [*(blocks[n] for n in range(Z // 2)), *last, *(blocks[n - Z // 2] for n in range(1, Z // 2))]
    else:
        ring = {(0, 0): kept, (1, 0): neighbours}

        def hop(other, behind):
            side = 1 if behind > 0 else -1
            ring[other, behind] = lax.ppermute(ring[other, behind - side], "z", forward if side > 0 else backward)

        for of in HOPS[:2]:
            hop(*of)
        packed = pack_amplitudes(amplitudes, occ_irrep, vir_irrep, slots)
        packed, ring[1, 0], ring[0, 1] = lax.optimization_barrier((packed, ring[1, 0], ring[0, 1]))
        for of in HOPS[2:]:
            hop(*of)
        ring = [ring[key][None] for key in RING]
    received = lax.all_to_all(
        packed.reshape(JA * YL, lane_tiles(slots) * PAIRS, LANES), ("ja", "yl"), split_axis=0, concat_axis=0, tiled=True
    ).reshape(JA, YL, lane_tiles(slots), PAIRS, LANES)
    occ_rows = lax.dynamic_slice_in_dim(occ_irrep, YL * NI * lax.axis_index("z"), YL * NI).reshape(YL, 1, NI, 1)
    labels = jnp.bitwise_xor(occ_rows, occ_irrep.reshape(1, JA, 1, NI)).reshape(YL, 1, ROWS)
    parts = contract(received, ring, labels, vir_irrep, slots, keep_all)
    parts = lax.all_to_all(
        parts.reshape((YL * JA,) + parts.shape[2:]), ("yl", "ja"), split_axis=0, concat_axis=0, tiled=True
    )
    return reduce_parts(parts, labels, vir_irrep, keep_all)


def tier_kernel(occ, vir, out_ref):
    def largest_class(ref):
        def count(n, counts):
            one = lax.shift_left(1, 8 * (ref[n] & 3))
            return counts[0] + jnp.where(ref[n] < 4, one, 0), counts[1] + jnp.where(ref[n] < 4, 0, one)

        counts = lax.fori_loop(0, ref.shape[0], count, (jnp.int32(0), jnp.int32(0)), unroll=True)
        largest = jnp.int32(0)
        for four in counts:
            for n in range(4):
                largest = jnp.maximum(largest, lax.shift_right_logical(four, 8 * n) & 255)
        return largest

    out_ref[0] = jnp.where(largest_class(occ) <= KEPT // NI, jnp.minimum(jnp.maximum(largest_class(vir) - 2, 0), 2), 2)


def local(amplitudes, integrals, occ_irrep, vir_irrep, occ_energy, vir_energy):
    scalars = pl.BlockSpec(memory_space=pltpu.SMEM)
    tier = pl.pallas_call(
        tier_kernel, out_shape=jax.ShapeDtypeStruct((1,), jnp.int32), in_specs=[scalars] * 2, out_specs=scalars
    )(occ_irrep, vir_irrep)
    branches = [functools.partial(ladder_rows, *of) for of in ((2, False, False), (3, True, False), (NVT, True, True))]
    ladder = lax.switch(tier[0], branches, amplitudes, integrals, occ_irrep, vir_irrep)
    return finish(ladder.reshape(JA, PAIRS, LANES), occ_energy, vir_energy)


def solution(mesh):
    parts = Mesh(mesh.devices.reshape(Z, YL, JA), ("z", "yl", "ja"))
    rows = ("z", "yl")
    in_specs = (P(rows, "ja", None, None), P(rows, "ja", None), P(), P(), P(), P())
    return jax.shard_map(local, mesh=parts, in_specs=in_specs, out_specs=P(rows, None, "ja"), check_vma=False)
```
